256 devices in a mesh: dp: 2 (over x_lo), space: 128 (over z, y, x_hi, core).
Axes of the slice: x: 4 (x_hi: 2, x_lo: 2; x = x_hi * 2 + x_lo), y: 4, z: 8, core: 2. Of those that a mesh axis runs over, the one named last changes fastest.
Arguments:
- latent: bfloat16 [2, 1024, 128, 512], P('dp', 'space'), may hold values from -6 to 6
- cotangent: bfloat16 [2, 1024, 128, 512], P('dp', 'space'), may hold values from -6 to 6
- w_qkv: bfloat16 [512, 1536], replicated, may hold values from -1.6840242 to 1.6840242
- w_out: bfloat16 [512, 512], replicated, may hold values from -0.25 to 0.25
- norm_gain: float32 [512], replicated, may hold values from 0.1 to 1.9
- norm_bias: float32 [512], replicated, may hold values from -3 to 3
Outputs:
- output: bfloat16 [2, 1024, 128, 512], P('dp', 'space')
- grad_input: bfloat16 [2, 1024, 128, 512], P('dp', 'space')
- grad_qkv: float32 [786432], P(('dp', 'space'))
- grad_out: float32 [262144], P(('dp', 'space'))
- grad_norm: float32 [2, 512], replicated
The draws below stay inside these ranges and needn't reach their ends.
All inputs are finite; a program needn't handle non-finite values.
Results may differ from the reference program's by a relative error of at most 0.015.
The reference program's roundings to bfloat16 on the way (of `normed`, `projected`, `grad_heads`, `probs_low`, `attended`, `grad_values`, `grad_scores` and `grad_proj`) count: a program that leaves them out, or rounds other values in their place, can miss the bound.
Values may be sent and summed in bfloat16 or wider, within the bound.
No kernel may reach another device: no remote copies, remote signals or barrier semaphores. Data moves between devices by JAX's collectives and lax.ppermute only.
A program may use at most 128 MiB of HBM per device.

```python
import math
import jax
import jax.numpy as jnp
from jax import lax

C = 512
HEADS = 16
GRID = 8
COLS = 128
ROWS = 1024
MEMBERS = 2


def draw_w_qkv(key, part):
    key = jax.random.fold_in(key, 7)
    first_key = jax.random.fold_in(key, 0)
    result = jnp.clip(jax.random.normal(first_key, (C, 3 * C), jnp.float32), -4.0, 4.0) / math.sqrt(C)
    return result.astype(jnp.bfloat16)


def level_of(stream_key, shape, shards, least, high):
    def one(axis_at, parts):
        draws = jax.random.uniform(jax.random.fold_in(jax.random.fold_in(stream_key, 6), axis_at), (parts,), jnp.float32, least / len(shards), high / len(shards))
        return jnp.repeat(jnp.exp(draws), shape[axis_at] // parts).reshape((-1,) + (1,) * (len(shape) - axis_at - 1))

    level = one(*shards[0])
    for cut in shards[1:]:
        level = level * one(*cut)
    return level


def normal_values(rng, dims, deviation, reach, cuts=(), kind=jnp.bfloat16):
    loudness = level_of(rng, dims, cuts, -0.22, 0.18) if cuts else 1.0
    drawn = jax.random.normal(rng, dims, jnp.float32) * deviation * loudness
    return jnp.minimum(jnp.maximum(drawn, -reach), reach).astype(kind)


def setup_inputs(seed: int = 0) -> dict:
    splits = jax.random.split(jax.random.key(seed), 7)
    return {
        "latent": normal_values(splits[0], (MEMBERS, ROWS, COLS, C), 1.0, 6.0, ((0, 2), (1, 128))),
        "cotangent": normal_values(splits[1], (MEMBERS, ROWS, COLS, C), 1.0, 6.0, ((0, 2), (1, 128))),
        "w_qkv": draw_w_qkv(jax.random.fold_in(splits[6], 71), 0),
        "w_out": normal_values(splits[3], (C, C), C ** -0.5, 0.25),
        "norm_gain": jnp.clip(1.0 + 0.18 * jax.random.normal(splits[4], (C,), jnp.float32), 0.1, 1.9),
        "norm_bias": normal_values(splits[5], (C,), 0.5, 3.0, (), jnp.float32),
    }


def norm_parts(values, norm_gain, norm_bias):
    center = lax.optimization_barrier(jnp.mean(values, -1, keepdims=True))
    offset = values - center
    variance = lax.optimization_barrier(jnp.mean(offset * offset, -1, keepdims=True))
    inverse = lax.rsqrt(variance + 1e-05)
    scaled = offset * inverse
    normed = (scaled * norm_gain + norm_bias).astype(jnp.bfloat16)
    return (scaled, inverse, normed)

def window_pass(projected, grad_heads):
    blocks, length, width = grad_heads.shape
    head_size = width // HEADS
    factor = 1.0 / math.sqrt(head_size)
    queries = projected[..., :width].reshape(blocks, length, HEADS, head_size).astype(jnp.float32)
    keys_all = projected[..., width:2 * width].reshape(blocks, length, HEADS, head_size).astype(jnp.float32)
    values_all = projected[..., 2 * width:].reshape(blocks, length, HEADS, head_size).astype(jnp.float32)
    grad_wide = grad_heads.reshape(blocks, length, HEADS, head_size).astype(jnp.float32)
    scores = jnp.einsum('bqhd,bkhd->bhqk', queries, keys_all) * factor
    highest = lax.optimization_barrier(jnp.max(scores, -1, keepdims=True))
    weights = jnp.exp(scores - highest)
    probs = weights / lax.optimization_barrier(jnp.sum(weights, -1, keepdims=True))
    probs_low = probs.astype(jnp.bfloat16).astype(jnp.float32)
    attended = jnp.einsum('bhqk,bkhd->bqhd', probs_low, values_all).astype(jnp.bfloat16)
    grad_probs = jnp.einsum('bqhd,bkhd->bhqk', grad_wide, values_all)
    grad_values = jnp.einsum('bhqk,bqhd->bkhd', probs_low, grad_wide).astype(jnp.bfloat16)
    grad_scores = (probs * (grad_probs - lax.optimization_barrier(jnp.sum(probs * grad_probs, -1, keepdims=True)))).astype(jnp.bfloat16).astype(jnp.float32)
    grad_queries = (jnp.einsum('bhqk,bkhd->bqhd', grad_scores, keys_all) * factor).astype(jnp.bfloat16)
    grad_keys = (jnp.einsum('bhqk,bqhd->bkhd', grad_scores, queries) * factor).astype(jnp.bfloat16)
    grad_proj = jnp.concatenate([grad_queries.reshape(blocks, length, width), grad_keys.reshape(blocks, length, width), grad_values.reshape(blocks, length, width)], -1)
    return (attended.reshape(blocks, length, width), grad_proj)

def reference(latent, cotangent, w_qkv, w_out, norm_gain, norm_bias):
    members, rows, columns, width = latent.shape
    flat_latent = latent.reshape(-1, width)
    flat_grad = cotangent.reshape(-1, width)
    scaled, inverse, normed = norm_parts(flat_latent.astype(jnp.float32), norm_gain, norm_bias)
    projected = jnp.dot(normed, w_qkv, preferred_element_type=jnp.float32).astype(jnp.bfloat16)
    grad_heads = lax.dot_general(flat_grad, w_out, (((1,), (1,)), ((), ())), preferred_element_type=jnp.float32).astype(jnp.bfloat16)

    def to_windows(tensor):
        depth = tensor.shape[-1]
        tensor = tensor.reshape(members, GRID, rows // GRID, GRID, columns // GRID, depth)
        tensor = tensor.transpose(0, 2, 4, 1, 3, 5)
        return tensor.reshape(members * (rows // GRID), columns // GRID, GRID * GRID, depth)

    def from_windows(tensor):
        depth = tensor.shape[-1]
        tensor = tensor.reshape(members, rows // GRID, columns // GRID, GRID, GRID, depth)
        tensor = tensor.transpose(0, 3, 1, 4, 2, 5)
        return tensor.reshape(members * rows * columns, depth)
    win_proj = to_windows(projected)
    win_grad = to_windows(grad_heads)
    attended_w, grad_proj_w = lax.map(lambda pair: window_pass(pair[0], pair[1]), (win_proj, win_grad))
    attended = from_windows(attended_w)
    grad_proj = from_windows(grad_proj_w)
    output = (flat_latent.astype(jnp.float32) + jnp.dot(attended, w_out, preferred_element_type=jnp.float32)).astype(jnp.bfloat16)
    term_out = lax.dot_general(attended, flat_grad, (((0,), (0,)), ((), ())), preferred_element_type=jnp.float32)
    term_qkv = lax.dot_general(normed, grad_proj, (((0,), (0,)), ((), ())), preferred_element_type=jnp.float32)
    grad_normed = lax.dot_general(grad_proj, w_qkv, (((1,), (1,)), ((), ())), preferred_element_type=jnp.float32)
    grad_hat = grad_normed * norm_gain
    grad_input = flat_grad.astype(jnp.float32) + inverse * (grad_hat - lax.optimization_barrier(jnp.mean(grad_hat, -1, keepdims=True)) - scaled * lax.optimization_barrier(jnp.mean(grad_hat * scaled, -1, keepdims=True)))
    grad_norm = jnp.stack([lax.optimization_barrier(jnp.sum(grad_normed * scaled, 0)), lax.optimization_barrier(jnp.sum(grad_normed, 0))])
    return (output.reshape(members, rows, columns, width), grad_input.astype(jnp.bfloat16).reshape(members, rows, columns, width), term_qkv.reshape(-1), term_out.reshape(-1), grad_norm)
```

```python
import functools
import math

import jax
import jax.numpy as jnp
from jax import lax
from jax.experimental import pallas as pl
from jax.experimental.pallas import tpu as pltpu
from jax.sharding import PartitionSpec as P

HEADS = 16
GRID = 8
CHUNKS = 2
BLOCK = 4
PACK = 4
VMEM_LIMIT = 56 * 1024 * 1024


def column_order(columns, transposed):
    inner = columns // GRID
    row = lax.broadcasted_iota(jnp.int32, (columns, columns), 0)
    col = lax.broadcasted_iota(jnp.int32, (columns, columns), 1)
    if transposed:
        row, col = col, row
    hit = (row // GRID == col % inner) & (row % GRID == col // inner)
    return jnp.where(hit, 1.0, 0.0).astype(jnp.bfloat16)


def pack_kernel(latent_ref, cotangent_ref, *out_refs):
    columns = latent_ref.shape[1]
    rows = columns // CHUNKS
    order = column_order(columns, False)
    for spot in range(GRID):
        for half, ref in enumerate((latent_ref, cotangent_ref)):
            moved = jnp.dot(order, ref[spot], preferred_element_type=jnp.float32)
            moved = moved.astype(jnp.bfloat16)
            for chunk in range(CHUNKS):
                out_refs[chunk][spot, half] = moved[chunk * rows : (chunk + 1) * rows]


def unpack_kernel(*refs):
    piece_refs = refs[:CHUNKS]
    output_ref, grad_ref = refs[CHUNKS:]
    columns = output_ref.shape[1]
    order = column_order(columns, True)
    for spot in range(GRID):
        for half, ref in enumerate((output_ref, grad_ref)):
            rows = jnp.concatenate([piece_ref[spot, half] for piece_ref in piece_refs], 0)
            moved = jnp.dot(order, rows, preferred_element_type=jnp.float32)
            ref[spot] = moved.astype(jnp.bfloat16)


def dot_nt(a, b):
    return lax.dot_general(a, b, (((1,), (1,)), ((), ())), preferred_element_type=jnp.float32)


def dot_tn(a, b):
    return lax.dot_general(a, b, (((0,), (0,)), ((), ())), preferred_element_type=jnp.float32)


def window_kernel(first, last, *refs):
    piece_ref, w_qkv_ref, w_out_ref, gain_ref, bias_ref = refs[:5]
    rest = refs[5:]
    if not first:
        old_qkv_ref, old_out_ref, old_norm_ref = rest[:3]
        rest = rest[3:]
    out_ref = rest[0]
    normed_ref, attended_ref, proj_ref, heads_ref, grad_ref, cot_ref = rest[-6:]
    if last:
        shares_ref = rest[1]
    else:
        grad_qkv_ref, grad_out_ref, grad_norm_ref = rest[1:4]
    width = w_out_ref.shape[0]
    head_size = width // HEADS
    factor = 1.0 / math.sqrt(head_size)
    lanes = PACK * head_size
    cells = GRID * GRID
    rows = piece_ref.shape[2]
    steps = rows // (BLOCK * GRID)
    span = BLOCK * cells

    lane_head = lax.broadcasted_iota(jnp.int32, (PACK * cells, lanes), 1) // head_size
    row_head = lax.broadcasted_iota(jnp.int32, (PACK * cells, lanes), 0) // cells
    own = jnp.where(lane_head == row_head, 1.0, 0.0).astype(jnp.bfloat16)
    lane_of = lax.broadcasted_iota(jnp.int32, (cells, lanes), 1) // head_size

    def spread(part):
        return jnp.concatenate([part] * PACK, 0) * own

    def gather_heads(wide):
        result = wide[:cells]
        for h in range(1, PACK):
            result = jnp.where(lane_of == h, wide[h * cells : (h + 1) * cells], result)
        return result

    def step(i, norm_sums):
        at = pl.multiple_of(i * (BLOCK * GRID), BLOCK * GRID)
        base = pl.multiple_of(i * span, span)

        def load(half):
            parts = [
                piece_ref[spot, half, pl.ds(at, BLOCK * GRID), :]
                .astype(jnp.float32)
                .reshape(BLOCK, GRID, width)
                for spot in range(GRID)
            ]
            return jnp.stack(parts, 1).reshape(span, width)

        latent = load(0)
        cotangent = load(1)
        center = jnp.mean(latent, -1, keepdims=True)
        offset = latent - center
        variance = jnp.mean(offset * offset, -1, keepdims=True)
        inverse = lax.rsqrt(variance + 1e-05)
        scaled = offset * inverse
        normed = (scaled * gain_ref[...] + bias_ref[...]).astype(jnp.bfloat16)
        cot_low = cotangent.astype(jnp.bfloat16)
        normed_ref[pl.ds(base, span), :] = normed
        cot_ref[pl.ds(base, span), :] = cot_low
        proj_ref[...] = jnp.dot(
            normed, w_qkv_ref[...], preferred_element_type=jnp.float32
        ).astype(jnp.bfloat16)
        heads_ref[...] = dot_nt(cot_low, w_out_ref[...]).astype(jnp.bfloat16)
        for w in range(BLOCK):
            own_rows = slice(w * cells, (w + 1) * cells)
            store_rows = pl.ds(base + w * cells, cells)
            for g in range(HEADS // PACK):
                lo = g * lanes
                queries = proj_ref[own_rows, lo : lo + lanes]
                keys = proj_ref[own_rows, width + lo : width + lo + lanes]
                values = proj_ref[own_rows, 2 * width + lo : 2 * width + lo + lanes]
                grads = heads_ref[own_rows, lo : lo + lanes]
                wide_q = spread(queries)
                wide_g = spread(grads)
                scores = dot_nt(keys, wide_q) * factor
                highest = jnp.max(scores, 0, keepdims=True)
                weights = jnp.exp(scores - highest)
                probs = weights / jnp.sum(weights, 0, keepdims=True)
                probs_low = probs.astype(jnp.bfloat16)
                grad_probs = dot_nt(values, wide_g)
                mean_grad = jnp.sum(probs * grad_probs, 0, keepdims=True)
                grad_scores = (probs * (grad_probs - mean_grad)).astype(jnp.bfloat16)
                attended = gather_heads(dot_tn(probs_low, values))
                grad_q = gather_heads(dot_tn(grad_scores, keys)) * factor
                grad_k = jnp.dot(grad_scores, wide_q, preferred_element_type=jnp.float32) * factor
                grad_v = jnp.dot(probs_low, wide_g, preferred_element_type=jnp.float32)
                attended_ref[store_rows, lo : lo + lanes] = attended.astype(jnp.bfloat16)
                grad_ref[store_rows, lo : lo + lanes] = grad_q.astype(jnp.bfloat16)
                grad_ref[store_rows, width + lo : width + lo + lanes] = grad_k.astype(jnp.bfloat16)
                grad_ref[store_rows, 2 * width + lo : 2 * width + lo + lanes] = grad_v.astype(
                    jnp.bfloat16
                )
        output = latent + jnp.dot(
            attended_ref[pl.ds(base, span), :], w_out_ref[...], preferred_element_type=jnp.float32
        )
        grad_normed = dot_nt(grad_ref[pl.ds(base, span), :], w_qkv_ref[...])
        grad_hat = grad_normed * gain_ref[...]
        grad_input = cotangent + inverse * (
            grad_hat
            - jnp.mean(grad_hat, -1, keepdims=True)
            - scaled * jnp.mean(grad_hat * scaled, -1, keepdims=True)
        )
        for half, value in enumerate((output, grad_input)):
            value = value.reshape(BLOCK, GRID, GRID, width)
            for s in range(GRID):
                piece = value[:, s].reshape(BLOCK * GRID, width)
                out_ref[s, half, pl.ds(at, BLOCK * GRID), :] = piece.astype(jnp.bfloat16)
        gain_sum = jnp.sum(grad_normed * scaled, 0, keepdims=True)
        bias_sum = jnp.sum(grad_normed, 0, keepdims=True)
        return (norm_sums[0] + gain_sum, norm_sums[1] + bias_sum)

    if first:
        start = (jnp.zeros((1, width), jnp.float32), jnp.zeros((1, width), jnp.float32))
    else:
        start = (old_norm_ref[0:1, :], old_norm_ref[1:2, :])
    sums = lax.fori_loop(0, steps, step, start)
    grad_qkv = dot_tn(normed_ref[...], grad_ref[...])
    grad_out = dot_tn(attended_ref[...], cot_ref[...])
    if not first:
        grad_qkv = grad_qkv + old_qkv_ref[...]
        grad_out = grad_out + old_out_ref[...]
    if not last:
        grad_norm_ref[0:1, :] = sums[0]
        grad_norm_ref[1:2, :] = sums[1]
        grad_qkv_ref[...] = grad_qkv
        grad_out_ref[...] = grad_out
        return
    low = jnp.bfloat16
    order = share_order(width, shares_ref.shape[0])
    for lo, part in ((0, grad_qkv), (3 * width, grad_out)):
        part = jnp.dot(order, part.astype(low), preferred_element_type=jnp.float32).astype(low)
        part = part.reshape(shares_ref.shape[0], shares_ref.shape[1], part.shape[1])
        shares_ref[:, :, lo : lo + part.shape[2]] = part
    norm = jnp.concatenate([s[:, i : i + 128] for s in sums for i in range(0, width, 128)], 0)
    high = norm.astype(low).astype(jnp.float32)
    norm = jnp.concatenate([high, norm - high], 0).astype(low)
    shares_ref[:, :, 4 * width :] = jnp.broadcast_to(norm[None], (shares_ref.shape[0],) + norm.shape)


def share_order(width, planes):
    pair = width // (planes * GRID)
    near = planes // 2
    row = lax.broadcasted_iota(jnp.int32, (width, width), 0)
    col = lax.broadcasted_iota(jnp.int32, (width, width), 1)
    at = row % pair
    spot = row // pair % GRID
    plane = row // (pair * GRID)
    source = ((plane // near * GRID + spot) * near + plane % near) * pair + at
    return jnp.where(col == source, 1.0, 0.0).astype(jnp.bfloat16)


def first_sum_kernel(shares_ref, out_ref):
    low = jnp.bfloat16
    total = jnp.sum(shares_ref[...].astype(jnp.float32), 0)
    rows, wide = total.shape
    count = rows // GRID
    main = wide - 128
    norm = total[:GRID, main:] + total[GRID:, main:]
    high = norm.astype(low).astype(jnp.float32)
    rest = norm - high
    high = jnp.concatenate([high[i : i + 1] for i in range(GRID)], 1)
    rest = jnp.concatenate([rest[i : i + 1] for i in range(GRID)], 1)
    norm = jnp.concatenate([high, rest], 0).astype(low)
    out_ref[:, :, :main] = total[:, :main].reshape(GRID, count, main).astype(low)
    out_ref[:, :, main:] = jnp.broadcast_to(norm[None], (GRID,) + norm.shape)


def second_sum_kernel(shares_ref, qkv_ref, out_ref, norm_ref):
    total = jnp.sum(shares_ref[...].astype(jnp.float32), 0)
    width = out_ref.shape[1]
    qkv_ref[...] = total[:, : 3 * width]
    out_ref[...] = total[:, 3 * width : 4 * width]
    norm = total[0:1, 4 * width :] + total[1:2, 4 * width :]
    norm_ref[0:1, :] = norm[:, :width]
    norm_ref[1:2, :] = norm[:, width:]


VMEM = pl.BlockSpec(memory_space=pltpu.VMEM)
PARAMS = pltpu.CompilerParams(vmem_limit_bytes=VMEM_LIMIT)


def pack(latent, cotangent):
    spots, columns, width = latent.shape
    piece = jax.ShapeDtypeStruct((spots, 2, columns // CHUNKS, width), jnp.bfloat16)
    return pl.pallas_call(
        pack_kernel,
        out_shape=[piece] * CHUNKS,
        in_specs=[VMEM] * 2,
        out_specs=[VMEM] * CHUNKS,
        compiler_params=PARAMS,
        name="pack",
    )(latent, cotangent)


def unpack(pieces, columns):
    spots, _, _, width = pieces[0].shape
    whole = jax.ShapeDtypeStruct((spots, columns, width), jnp.bfloat16)
    return pl.pallas_call(
        unpack_kernel,
        out_shape=[whole] * 2,
        in_specs=[VMEM] * CHUNKS,
        out_specs=[VMEM] * 2,
        compiler_params=PARAMS,
        name="unpack",
    )(*pieces)


def windows(pieces, w_qkv, w_out, gain, bias, old, last):
    _, _, rows, width = pieces.shape
    tokens = GRID * rows
    span = BLOCK * GRID * GRID
    low = jnp.bfloat16
    flops = 2 * tokens * width * width * 12 + 6 * 2 * tokens * width * GRID * GRID * PACK
    if last:
        sums = [jax.ShapeDtypeStruct((last, width // last, 4 * width + 128), low)]
    else:
        sums = [
            jax.ShapeDtypeStruct((width, 3 * width), jnp.float32),
            jax.ShapeDtypeStruct((width, width), jnp.float32),
            jax.ShapeDtypeStruct((2, width), jnp.float32),
        ]
    return pl.pallas_call(
        functools.partial(window_kernel, not old, last),
        out_shape=[jax.ShapeDtypeStruct(pieces.shape, low)] + sums,
        in_specs=[VMEM] * (5 + len(old)),
        out_specs=[VMEM] * (1 + len(sums)),
        scratch_shapes=[
            pltpu.VMEM((tokens, width), low),
            pltpu.VMEM((tokens, width), low),
            pltpu.VMEM((span, 3 * width), low),
            pltpu.VMEM((span, width), low),
            pltpu.VMEM((tokens, 3 * width), low),
            pltpu.VMEM((tokens, width), low),
        ],
        compiler_params=PARAMS,
        cost_estimate=pl.CostEstimate(
            flops=flops, bytes_accessed=12 * 2**20, transcendentals=tokens * HEADS * GRID * GRID
        ),
        name="windows",
    )(pieces, w_qkv, w_out, gain, bias, *old)


def first_sum(shares):
    _, rows, wide = shares.shape
    result = jax.ShapeDtypeStruct((GRID, rows // GRID, wide - 128 + GRID * 128), jnp.bfloat16)
    return pl.pallas_call(
        first_sum_kernel,
        out_shape=result,
        in_specs=[VMEM],
        out_specs=VMEM,
        compiler_params=PARAMS,
        name="first_sum",
    )(shares)


def second_sum(shares, width):
    _, rows, _ = shares.shape
    return pl.pallas_call(
        second_sum_kernel,
        out_shape=[
            jax.ShapeDtypeStruct((rows, 3 * width), jnp.float32),
            jax.ShapeDtypeStruct((rows, width), jnp.float32),
            jax.ShapeDtypeStruct((2, width), jnp.float32),
        ],
        in_specs=[VMEM],
        out_specs=[VMEM] * 3,
        compiler_params=PARAMS,
        name="second_sum",
    )(shares)


PLANE = ("dp", "y", "x_hi", "core")


def swap(value, axes):
    return lax.all_to_all(value, axes, split_axis=0, concat_axis=0, tiled=True)


def body(latent, cotangent, w_qkv, w_out, norm_gain, norm_bias):
    _, _, columns, width = latent.shape
    planes = math.prod(lax.axis_size(name) for name in PLANE)
    pieces = pack(latent[0], cotangent[0])
    gain = norm_gain.reshape(1, width)
    bias = norm_bias.reshape(1, width)
    arrived = []
    for piece in pieces:
        if arrived:
            arrived[-1], piece = lax.optimization_barrier((arrived[-1], piece))
        arrived.append(swap(piece, "z"))
    sums = []
    returned = []
    for chunk in range(CHUNKS):
        result, *sums = windows(
            arrived[chunk], w_qkv, w_out, gain, bias, sums, planes if chunk == CHUNKS - 1 else 0
        )
        if returned:
            returned[-1], result = lax.optimization_barrier((returned[-1], result))
        returned.append(swap(result, "z"))
    shares = first_sum(swap(sums[0], PLANE))
    grad_qkv, grad_out, grad_norm = second_sum(swap(shares, "z"), width)
    output, grad_input = unpack(returned, columns)
    return (output[None], grad_input[None], grad_qkv.reshape(-1), grad_out.reshape(-1), grad_norm)


def solution(mesh):
    sizes = (mesh.shape["dp"], GRID, mesh.shape["space"] // GRID // 4, 2, 2)
    parts = jax.sharding.Mesh(mesh.devices.reshape(sizes), ("dp", "z", "y", "x_hi", "core"))
    space = ("z", "y", "x_hi", "core")
    in_specs = (P("dp", space, None, None), P("dp", space, None, None), P(), P(), P(), P())
    out_specs = (
        P("dp", space, None, None),
        P("dp", space, None, None),
        P(("dp",) + space),
        P(("dp",) + space),
        P(),
    )
    return jax.shard_map(body, mesh=parts, in_specs=in_specs, out_specs=out_specs, check_vma=False)
```

```python
import functools
import math

import jax
import jax.numpy as jnp
from jax import lax
from jax.experimental import pallas as pl
from jax.experimental.pallas import tpu as pltpu
from jax.sharding import PartitionSpec as P

HEADS = 16
GRID = 8
STEPS = 2
PACK = 4
UNROLL = 4
VMEM_LIMIT = 56 * 1024 * 1024
SMALL_LIMIT = 12 * 1024 * 1024
LOW = jnp.bfloat16
NEAR = (1, 7)


def dot_nn(a, b):
    return jnp.dot(a, b, preferred_element_type=jnp.float32)


def dot_nt(a, b):
    return lax.dot_general(a, b, (((1,), (1,)), ((), ())), preferred_element_type=jnp.float32)


def dot_tn(a, b):
    return lax.dot_general(a, b, (((0,), (0,)), ((), ())), preferred_element_type=jnp.float32)


def column_order(columns, back):
    inner = columns // GRID
    row = lax.broadcasted_iota(jnp.int32, (columns, columns), 0)
    col = lax.broadcasted_iota(jnp.int32, (columns, columns), 1)
    if back:
        row, col = col, row
    hit = (row // GRID == col % inner) & (row % GRID == col // inner)
    return jnp.where(hit, 1.0, 0.0).astype(LOW)


def to_windows(slabs_ref, cells_ref):
    spots, columns, width = slabs_ref.shape
    order = column_order(columns, False)
    for a in range(spots):
        moved = dot_nn(order, slabs_ref[a])
        cells_ref[:, a] = moved.reshape(columns // GRID, GRID, width)


def from_windows(cells_ref, a):
    inner, _, side, width = cells_ref.shape
    moved = cells_ref[:, a].reshape(inner * side, width).astype(LOW)
    return dot_nn(column_order(inner * side, True), moved).astype(LOW)


def step_rows(cells_ref, step):
    inner, spots, side, width = cells_ref.shape
    part = inner // STEPS
    return cells_ref[step * part : (step + 1) * part].reshape(part * spots * side, width)


def put_rows(cells_ref, step, value):
    inner, spots, side, width = cells_ref.shape
    part = inner // STEPS
    cells_ref[step * part : (step + 1) * part] = value.reshape(part, spots, side, width)


def norm_parts(values):
    center = jnp.mean(values, -1, keepdims=True)
    offset = values - center
    variance = jnp.mean(offset * offset, -1, keepdims=True)
    inverse = lax.rsqrt(variance + 1e-05)
    return offset * inverse, inverse


class Heads:
    def __init__(self, width):
        self.head_size = width // HEADS
        self.lanes = PACK * self.head_size
        self.cells = GRID * GRID
        self.factor = 1.0 / math.sqrt(self.head_size)
        shape = (PACK * self.cells, self.lanes)
        lane_head = lax.broadcasted_iota(jnp.int32, shape, 1) // self.head_size
        row_head = lax.broadcasted_iota(jnp.int32, shape, 0) // self.cells
        self.own = jnp.where(lane_head == row_head, 1.0, 0.0).astype(LOW)
        self.lane_of = lax.broadcasted_iota(jnp.int32, (self.cells, self.lanes), 1) // self.head_size
        self.slices = [slice(g * self.lanes, (g + 1) * self.lanes) for g in range(HEADS // PACK)]

    def spread(self, part):
        return jnp.concatenate([part] * PACK, 0) * self.own

    def gather(self, wide):
        result = wide[: self.cells]
        for h in range(1, PACK):
            result = jnp.where(self.lane_of == h, wide[h * self.cells : (h + 1) * self.cells], result)
        return result

    def probs(self, keys, wide_q):
        scores = [dot_nt(k, q) * self.factor for k, q in zip(keys, wide_q)]
        weights = [jnp.exp(s - jnp.max(s, 0, keepdims=True)) for s in scores]
        return [e * (1.0 / jnp.sum(e, 0, keepdims=True)) for e in weights]


def forward_kernel(slabs_ref, w_qkv_ref, w_out_ref, gain_ref, bias_ref, *refs):
    piece_refs = refs[:GRID]
    latent_ref, proj_ref, attended_ref, cells_ref = refs[GRID:]
    width = w_out_ref.shape[0]
    rows = latent_ref.shape[0] // STEPS
    to_windows(slabs_ref, cells_ref)
    for step in range(STEPS):
        at = slice(step * rows, (step + 1) * rows)
        latent = step_rows(cells_ref, step)
        latent_ref[at, :] = latent.astype(LOW)
        scaled, _ = norm_parts(latent)
        normed = (scaled * gain_ref[...] + bias_ref[...]).astype(LOW)
        proj_ref[at, :] = dot_nn(normed, w_qkv_ref[...]).astype(LOW)
    heads = Heads(width)

    def window(w, carry):
        at = pl.ds(pl.multiple_of(w * heads.cells, heads.cells), heads.cells)
        keys = [proj_ref[at, width + s.start : width + s.stop] for s in heads.slices]
        wide_q = [heads.spread(proj_ref[at, s]) for s in heads.slices]
        probs = [p.astype(LOW) for p in heads.probs(keys, wide_q)]
        for s, p in zip(heads.slices, probs):
            values = proj_ref[at, 2 * width + s.start : 2 * width + s.stop]
            attended_ref[at, s] = heads.gather(dot_tn(p, values)).astype(LOW)
        return carry

    lax.fori_loop(0, latent_ref.shape[0] // heads.cells, window, 0, unroll=UNROLL)
    for step in range(STEPS):
        at = slice(step * rows, (step + 1) * rows)
        value = step_rows(cells_ref, step) + dot_nn(attended_ref[at, :], w_out_ref[...])
        put_rows(cells_ref, step, value)
    spot = lax.axis_index("z")
    for shift in range(GRID):
        piece_refs[shift][...] = from_windows(cells_ref, lax.rem(spot + GRID - shift, GRID))


def backward_kernel(
    slabs_ref, latent_ref, proj_ref, attended_ref, w_qkv_ref, w_out_ref, gain_ref, bias_ref, *refs
):
    near_refs, piece_refs = refs[:2], refs[2 : 2 + GRID]
    keep_ref, send_ref, cells_ref, cot_ref, heads_ref, grad_ref, normed_ref = refs[2 + GRID :]
    width = w_out_ref.shape[0]
    rows = latent_ref.shape[0] // STEPS
    to_windows(slabs_ref, cells_ref)
    for step in range(STEPS):
        at = slice(step * rows, (step + 1) * rows)
        cot_ref[at, :] = step_rows(cells_ref, step).astype(LOW)
        heads_ref[at, :] = dot_nt(cot_ref[at, :], w_out_ref[...]).astype(LOW)
    heads = Heads(width)

    def window(w, carry):
        at = pl.ds(pl.multiple_of(w * heads.cells, heads.cells), heads.cells)
        keys = [proj_ref[at, width + s.start : width + s.stop] for s in heads.slices]
        values = [proj_ref[at, 2 * width + s.start : 2 * width + s.stop] for s in heads.slices]
        wide_q = [heads.spread(proj_ref[at, s]) for s in heads.slices]
        wide_g = [heads.spread(heads_ref[at, s]) for s in heads.slices]
        grad_probs = [dot_nt(v, g) for v, g in zip(values, wide_g)]
        probs = heads.probs(keys, wide_q)
        grad_scores = [
            (p * (d - jnp.sum(p * d, 0, keepdims=True))).astype(LOW)
            for p, d in zip(probs, grad_probs)
        ]
        for i, s in enumerate(heads.slices):
            grad_v = dot_nn(probs[i].astype(LOW), wide_g[i])
            grad_k = dot_nn(grad_scores[i], wide_q[i]) * heads.factor
            grad_q = heads.gather(dot_tn(grad_scores[i], keys[i])) * heads.factor
            for j, part in enumerate((grad_q, grad_k, grad_v)):
                grad_ref[at, j * width + s.start : j * width + s.stop] = part.astype(LOW)
        return carry

    lax.fori_loop(0, latent_ref.shape[0] // heads.cells, window, 0, unroll=UNROLL)
    gain_sum = jnp.zeros((1, width), jnp.float32)
    bias_sum = jnp.zeros((1, width), jnp.float32)
    for step in range(STEPS):
        at = slice(step * rows, (step + 1) * rows)
        scaled, inverse = norm_parts(latent_ref[at, :].astype(jnp.float32))
        normed_ref[at, :] = (scaled * gain_ref[...] + bias_ref[...]).astype(LOW)
        grad_normed = dot_nt(grad_ref[at, :], w_qkv_ref[...])
        gain_sum += jnp.sum(grad_normed * scaled, 0, keepdims=True)
        bias_sum += jnp.sum(grad_normed, 0, keepdims=True)
        grad_hat = grad_normed * gain_ref[...]
        value = step_rows(cells_ref, step) + inverse * (
            grad_hat
            - jnp.mean(grad_hat, -1, keepdims=True)
            - scaled * jnp.mean(grad_hat * scaled, -1, keepdims=True)
        )
        put_rows(cells_ref, step, value)
    spot = lax.axis_index("z")
    for shift in range(GRID):
        piece = from_windows(cells_ref, lax.rem(spot + GRID - shift, GRID))
        if shift in NEAR:
            piece_refs[shift][0] = near_refs[NEAR.index(shift)][...]
            piece_refs[shift][1] = piece
        else:
            piece_refs[shift][...] = piece
    norm = [s[:, i : i + 128] for s in (gain_sum, bias_sum) for i in range(0, width, 128)]
    norm = jnp.concatenate(norm, 0)
    high = norm.astype(LOW).astype(jnp.float32)
    norm = jnp.concatenate([high, norm - high], 0).astype(LOW)
    parts = [
        (0, dot_tn(normed_ref[...], grad_ref[...]).astype(LOW)),
        (3 * width, dot_tn(attended_ref[...], cot_ref[...]).astype(LOW)),
    ]
    planes, share, _ = keep_ref.shape
    core = lax.axis_index("core")
    for ref, core_at in ((keep_ref, core), (send_ref, 1 - core)):
        order = share_order(width, planes, core_at)
        for lo, part in parts:
            part = dot_nn(order, part).astype(LOW).reshape(planes, share, part.shape[1])
            ref[:, :, lo : lo + part.shape[2]] = part
        ref[:, :, 4 * width :] = jnp.broadcast_to(norm[None], (planes,) + norm.shape)


def share_order(width, planes, core):
    pair = width // (2 * planes * GRID)
    near = planes // 2
    row = lax.broadcasted_iota(jnp.int32, (width // 2, width), 0)
    col = lax.broadcasted_iota(jnp.int32, (width // 2, width), 1)
    plane = row // (pair * GRID)
    spot = row // pair % GRID
    source = (((plane // near * GRID + spot) * near + plane % near) * 2 + core) * pair + row % pair
    return jnp.where(col == source, 1.0, 0.0).astype(LOW)


def first_sum_kernel(shares_ref, out_ref):
    total = jnp.sum(shares_ref[...].astype(jnp.float32), 0)
    rows, wide = total.shape
    count = rows // GRID
    main = wide - 128
    norm = total[:GRID, main:] + total[GRID:, main:]
    high = norm.astype(LOW).astype(jnp.float32)
    rest = norm - high
    high = jnp.concatenate([high[i : i + 1] for i in range(GRID)], 1)
    rest = jnp.concatenate([rest[i : i + 1] for i in range(GRID)], 1)
    norm = jnp.concatenate([high, rest], 0).astype(LOW)
    out_ref[:, :, :main] = total[:, :main].reshape(GRID, count, main).astype(LOW)
    out_ref[:, :, main:] = jnp.broadcast_to(norm[None], (GRID,) + norm.shape)


def second_sum_kernel(shares_ref, qkv_ref, out_ref, norm_ref):
    total = jnp.sum(shares_ref[...].astype(jnp.float32), 0)
    width = norm_ref.shape[1]
    for row in range(total.shape[0]):
        qkv_ref[row * 3 * width : (row + 1) * 3 * width] = total[row, : 3 * width]
        out_ref[row * width : (row + 1) * width] = total[row, 3 * width : 4 * width]
    norm = total[0:1, 4 * width :] + total[1:2, 4 * width :]
    norm_ref[0:1, :] = norm[:, :width]
    norm_ref[1:2, :] = norm[:, width:]


def gather_kernel(*refs):
    spot = lax.axis_index("z")
    out_ref, grad_ref = refs[2 * GRID - 2 :]
    near = [refs[NEAR.index(shift)] if shift in NEAR else None for shift in range(GRID)]
    rest = list(refs[2 : 2 * GRID - 2])
    for shift in range(GRID):
        at = lax.rem(spot + shift, GRID)
        if shift in NEAR:
            out_ref[at] = near[shift][0]
            grad_ref[at] = near[shift][1]
        else:
            out_ref[at] = rest.pop(0)[...]
            grad_ref[at] = rest.pop(0)[...]


VMEM = pl.BlockSpec(memory_space=pltpu.VMEM)
SHAPE = jax.ShapeDtypeStruct


def call(kernel, name, out_shape, *args, scratch=(), flops=0, moved=0, exps=0, limit=SMALL_LIMIT):
    return pl.pallas_call(
        kernel,
        out_shape=out_shape,
        in_specs=[VMEM] * len(args),
        out_specs=jax.tree.map(lambda _: VMEM, out_shape),
        scratch_shapes=list(scratch),
        compiler_params=pltpu.CompilerParams(vmem_limit_bytes=limit),
        cost_estimate=pl.CostEstimate(flops=flops, bytes_accessed=moved, transcendentals=exps),
        name=name,
    )(*args)


def forward(slabs, w_qkv, w_out, gain, bias):
    spots, columns, width = slabs.shape
    tokens = spots * columns
    flops = 2 * tokens * width * (4 * width + 2 * GRID * GRID * PACK)
    return call(
        forward_kernel,
        "forward",
        [SHAPE((columns, width), LOW)] * spots
        + [
            SHAPE((tokens, width), LOW),
            SHAPE((tokens, 3 * width), LOW),
            SHAPE((tokens, width), LOW),
        ],
        slabs,
        w_qkv,
        w_out,
        gain,
        bias,
        scratch=[pltpu.VMEM((columns // GRID, spots, GRID, width), jnp.float32)],
        flops=flops,
        moved=10 * 2**20,
        exps=tokens * HEADS * GRID * GRID,
        limit=VMEM_LIMIT,
    )


def backward(slabs, saved, near, w_qkv, w_out, gain, bias, planes):
    spots, columns, width = slabs.shape
    tokens = spots * columns
    share = width // (2 * planes)
    wide = 4 * width + 128
    flops = 2 * tokens * width * (9 * width + 5 * GRID * GRID * PACK)
    results = call(
        backward_kernel,
        "backward",
        [
            SHAPE(((2,) if shift in NEAR else ()) + (columns, width), LOW)
            for shift in range(spots)
        ]
        + [SHAPE((planes, share, wide), LOW)] * 2,
        slabs,
        *saved,
        w_qkv,
        w_out,
        gain,
        bias,
        *near,
        scratch=[
            pltpu.VMEM((columns // GRID, spots, GRID, width), jnp.float32),
            pltpu.VMEM((tokens, width), LOW),
            pltpu.VMEM((tokens, width), LOW),
            pltpu.VMEM((tokens, 3 * width), LOW),
            pltpu.VMEM((tokens, width), LOW),
        ],
        flops=flops,
        moved=16 * 2**20,
        exps=tokens * HEADS * GRID * GRID,
        limit=VMEM_LIMIT,
    )
    return results[:spots], results[spots:]


def first_sum(shares):
    _, rows, wide = shares.shape
    result = SHAPE((GRID, rows // GRID, wide - 128 + GRID * 128), LOW)
    return call(first_sum_kernel, "first_sum", result, shares)


def second_sum(shares, width):
    _, rows, _ = shares.shape
    result = [
        SHAPE((rows * 3 * width,), jnp.float32),
        SHAPE((rows * width,), jnp.float32),
        SHAPE((2, width), jnp.float32),
    ]
    return call(second_sum_kernel, "second_sum", result, shares)


def gather_slabs(outs, grads):
    columns, width = outs[0].shape
    pairs = [part for shift in range(GRID) if shift not in NEAR for part in (outs[shift], grads[shift])]
    near = [grads[shift] for shift in NEAR]
    return call(gather_kernel, "gather_slabs", [SHAPE((GRID, columns, width), LOW)] * 2, *near, *pairs)


def swap(value, axes):
    return lax.all_to_all(value, axes, split_axis=0, concat_axis=0, tiled=True)


def turn(value, shift):
    if shift % GRID == 0:
        return value
    return lax.ppermute(value, "z", [(a, (a + shift) % GRID) for a in range(GRID)])


def add(a, b):
    return (a.astype(jnp.float32) + b.astype(jnp.float32)).astype(LOW)


def body(latent, cotangent, w_qkv, w_out, norm_gain, norm_bias):
    width = latent.shape[-1]
    planes = lax.axis_size("dp") * lax.axis_size("y") * lax.axis_size("x_hi")
    gain = norm_gain.reshape(1, width)
    bias = norm_bias.reshape(1, width)
    slabs, cotangent = lax.optimization_barrier((swap(latent[0], "z"), cotangent[0]))
    cotangent = swap(cotangent, "z")
    results = forward(slabs, w_qkv, w_out, gain, bias)
    outs, saved = list(results[:GRID]), results[GRID:]
    near = [outs[shift] for shift in NEAR]
    outs = [piece if shift in NEAR else turn(piece, -shift) for shift, piece in enumerate(outs)]
    grads, (keep, send) = backward(cotangent, saved, near, w_qkv, w_out, gain, bias, planes)
    outs, keep, send = lax.optimization_barrier((outs, keep, send))
    grads = [turn(piece, -shift) for shift, piece in enumerate(grads)]
    shares = add(keep, lax.ppermute(send, "core", [(0, 1), (1, 0)]))
    grads[2], grads[6], shares = lax.optimization_barrier((grads[2], grads[6], shares))
    shares = first_sum(swap(shares, ("dp", "y", "x_hi")))
    grads[3:6], shares = lax.optimization_barrier((grads[3:6], shares))
    grad_qkv, grad_out, grad_norm = second_sum(swap(shares, "z"), width)
    output, grad_input = gather_slabs(outs, grads)
    return (output[None], grad_input[None], grad_qkv, grad_out, grad_norm)


def solution(mesh):
    sizes = (mesh.shape["dp"], GRID, mesh.shape["space"] // GRID // 4, 2, 2)
    parts = jax.sharding.Mesh(mesh.devices.reshape(sizes), ("dp", "z", "y", "x_hi", "core"))
    space = ("z", "y", "x_hi", "core")
    in_specs = (P("dp", space, None, None), P("dp", space, None, None), P(), P(), P(), P())
    out_specs = (
        P("dp", space, None, None),
        P("dp", space, None, None),
        P(("dp",) + space),
        P(("dp",) + space),
        P(),
    )
    return jax.shard_map(body, mesh=parts, in_specs=in_specs, out_specs=out_specs, check_vma=False)
```

```python
import functools
import math

import jax
import jax.numpy as jnp
from jax import lax
from jax.experimental import pallas as pl
from jax.experimental.pallas import tpu as pltpu
from jax.sharding import PartitionSpec as P

HEADS = 16
GRID = 8
STEPS = 2
PACK = 4
UNROLL = 8
VMEM_LIMIT = 56 * 1024 * 1024
SMALL_LIMIT = 12 * 1024 * 1024
LOW = jnp.bfloat16


def dot_nn(a, b):
    return jnp.dot(a, b, preferred_element_type=jnp.float32)


def dot_nt(a, b):
    return lax.dot_general(a, b, (((1,), (1,)), ((), ())), preferred_element_type=jnp.float32)


def dot_tn(a, b):
    return lax.dot_general(a, b, (((0,), (0,)), ((), ())), preferred_element_type=jnp.float32)


def column_order(columns, back):
    inner = columns // GRID
    row = lax.broadcasted_iota(jnp.int32, (columns, columns), 0)
    col = lax.broadcasted_iota(jnp.int32, (columns, columns), 1)
    if back:
        row, col = col, row
    hit = (row // GRID == col % inner) & (row % GRID == col // inner)
    return jnp.where(hit, 1.0, 0.0).astype(LOW)


def to_windows(slabs_ref, cells_ref):
    spots, columns, width = slabs_ref.shape
    order = column_order(columns, False)
    for a in range(spots):
        moved = dot_nn(order, slabs_ref[a])
        cells_ref[:, a] = moved.reshape(columns // GRID, GRID, width)


def from_windows(cells_ref, a):
    inner, _, side, width = cells_ref.shape
    moved = cells_ref[:, a].reshape(inner * side, width).astype(LOW)
    return dot_nn(column_order(inner * side, True), moved).astype(LOW)


def step_rows(cells_ref, step):
    inner, spots, side, width = cells_ref.shape
    part = inner // STEPS
    return cells_ref[step * part : (step + 1) * part].reshape(part * spots * side, width)


def put_rows(cells_ref, step, value):
    inner, spots, side, width = cells_ref.shape
    part = inner // STEPS
    cells_ref[step * part : (step + 1) * part] = value.reshape(part, spots, side, width)


def norm_parts(values):
    center = jnp.mean(values, -1, keepdims=True)
    offset = values - center
    variance = jnp.mean(offset * offset, -1, keepdims=True)
    inverse = lax.rsqrt(variance + 1e-05)
    return offset * inverse, inverse


class Heads:
    def __init__(self, width):
        self.head_size = width // HEADS
        self.lanes = PACK * self.head_size
        self.cells = GRID * GRID
        self.factor = 1.0 / math.sqrt(self.head_size)
        shape = (PACK * self.cells, self.lanes)
        lane_head = lax.broadcasted_iota(jnp.int32, shape, 1) // self.head_size
        row_head = lax.broadcasted_iota(jnp.int32, shape, 0) // self.cells
        self.own = jnp.where(lane_head == row_head, 1.0, 0.0).astype(LOW)
        self.lane_of = lax.broadcasted_iota(jnp.int32, (self.cells, self.lanes), 1) // self.head_size
        self.slices = [slice(g * self.lanes, (g + 1) * self.lanes) for g in range(HEADS // PACK)]

    def spread(self, part):
        return jnp.concatenate([part] * PACK, 0) * self.own

    def gather(self, wide):
        result = wide[: self.cells]
        for h in range(1, PACK):
            result = jnp.where(self.lane_of == h, wide[h * self.cells : (h + 1) * self.cells], result)
        return result

    def probs(self, keys, wide_q):
        scores = [dot_nt(k, q) * self.factor for k, q in zip(keys, wide_q)]
        weights = [jnp.exp(s - jnp.max(s, 0, keepdims=True)) for s in scores]
        return [e * (1.0 / jnp.sum(e, 0, keepdims=True)) for e in weights]


def forward_kernel(slabs_ref, w_qkv_ref, w_out_ref, gain_ref, bias_ref, *refs):
    piece_refs = refs[:GRID]
    latent_ref, proj_ref, attended_ref, cells_ref = refs[GRID:]
    width = w_out_ref.shape[0]
    rows = latent_ref.shape[0] // STEPS
    to_windows(slabs_ref, cells_ref)
    for step in range(STEPS):
        at = slice(step * rows, (step + 1) * rows)
        latent = step_rows(cells_ref, step)
        latent_ref[at, :] = latent.astype(LOW)
        scaled, _ = norm_parts(latent)
        normed = (scaled * gain_ref[...] + bias_ref[...]).astype(LOW)
        proj_ref[at, :] = dot_nn(normed, w_qkv_ref[...]).astype(LOW)
    heads = Heads(width)

    def window(w, carry):
        at = pl.ds(pl.multiple_of(w * heads.cells, heads.cells), heads.cells)
        keys = [proj_ref[at, width + s.start : width + s.stop] for s in heads.slices]
        wide_q = [heads.spread(proj_ref[at, s]) for s in heads.slices]
        probs = [p.astype(LOW) for p in heads.probs(keys, wide_q)]
        for s, p in zip(heads.slices, probs):
            values = proj_ref[at, 2 * width + s.start : 2 * width + s.stop]
            attended_ref[at, s] = heads.gather(dot_tn(p, values)).astype(LOW)
        return carry

    lax.fori_loop(0, latent_ref.shape[0] // heads.cells, window, 0, unroll=UNROLL)
    for step in range(STEPS):
        at = slice(step * rows, (step + 1) * rows)
        value = step_rows(cells_ref, step) + dot_nn(attended_ref[at, :], w_out_ref[...])
        put_rows(cells_ref, step, value)
    spot = lax.axis_index("z")
    for shift in range(GRID):
        piece_refs[shift][...] = from_windows(cells_ref, lax.rem(spot + GRID - shift, GRID))


def backward_kernel(
    slabs_ref, latent_ref, proj_ref, attended_ref, w_qkv_ref, w_out_ref, gain_ref, bias_ref, *refs
):
    hbm_refs = (slabs_ref, w_out_ref, proj_ref, latent_ref, w_qkv_ref, attended_ref)
    out_hbm_ref, keep_hbm_ref, send_hbm_ref = refs[:3]
    cells_ref, cot_ref, heads_ref, grad_ref, normed_ref = refs[3:8]
    vmem_refs = refs[8:14]
    out_ref, keep_ref, send_ref, in_sems, out_sems = refs[14:]
    slabs_ref, w_out_ref, proj_ref, latent_ref, w_qkv_ref, attended_ref = vmem_refs
    loads = [
        pltpu.make_async_copy(source, target, in_sems.at[i])
        for i, (source, target) in enumerate(zip(hbm_refs, vmem_refs))
    ]
    for load in loads:
        load.start()
    slabs_load, w_out_load, proj_load, latent_load, w_qkv_load, attended_load = loads
    width = w_out_ref.shape[0]
    rows = latent_ref.shape[0] // STEPS
    slabs_load.wait()
    to_windows(slabs_ref, cells_ref)
    w_out_load.wait()
    for step in range(STEPS):
        at = slice(step * rows, (step + 1) * rows)
        cot_ref[at, :] = step_rows(cells_ref, step).astype(LOW)
        heads_ref[at, :] = dot_nt(cot_ref[at, :], w_out_ref[...]).astype(LOW)
    proj_load.wait()
    heads = Heads(width)

    def window(w, carry):
        at = pl.ds(pl.multiple_of(w * heads.cells, heads.cells), heads.cells)
        keys = [proj_ref[at, width + s.start : width + s.stop] for s in heads.slices]
        values = [proj_ref[at, 2 * width + s.start : 2 * width + s.stop] for s in heads.slices]
        wide_q = [heads.spread(proj_ref[at, s]) for s in heads.slices]
        wide_g = [heads.spread(heads_ref[at, s]) for s in heads.slices]
        grad_probs = [dot_nt(v, g) for v, g in zip(values, wide_g)]
        probs = heads.probs(keys, wide_q)
        grad_scores = [
            (p * (d - jnp.sum(p * d, 0, keepdims=True))).astype(LOW)
            for p, d in zip(probs, grad_probs)
        ]
        for i, s in enumerate(heads.slices):
            grad_v = dot_nn(probs[i].astype(LOW), wide_g[i])
            grad_k = dot_nn(grad_scores[i], wide_q[i]) * heads.factor
            grad_q = heads.gather(dot_tn(grad_scores[i], keys[i])) * heads.factor
            for j, part in enumerate((grad_q, grad_k, grad_v)):
                grad_ref[at, j * width + s.start : j * width + s.stop] = part.astype(LOW)
        return carry

    lax.fori_loop(0, latent_ref.shape[0] // heads.cells, window, 0, unroll=UNROLL)
    latent_load.wait()
    w_qkv_load.wait()
    gain_sum = jnp.zeros((1, width), jnp.float32)
    bias_sum = jnp.zeros((1, width), jnp.float32)
    for step in range(STEPS):
        at = slice(step * rows, (step + 1) * rows)
        scaled, inverse = norm_parts(latent_ref[at, :].astype(jnp.float32))
        normed_ref[at, :] = (scaled * gain_ref[...] + bias_ref[...]).astype(LOW)
        grad_normed = dot_nt(grad_ref[at, :], w_qkv_ref[...])
        gain_sum += jnp.sum(grad_normed * scaled, 0, keepdims=True)
        bias_sum += jnp.sum(grad_normed, 0, keepdims=True)
        grad_hat = grad_normed * gain_ref[...]
        value = step_rows(cells_ref, step) + inverse * (
            grad_hat
            - jnp.mean(grad_hat, -1, keepdims=True)
            - scaled * jnp.mean(grad_hat * scaled, -1, keepdims=True)
        )
        put_rows(cells_ref, step, value)
    for a in range(GRID):
        out_ref[a] = from_windows(cells_ref, a)
    out_store = pltpu.make_async_copy(out_ref, out_hbm_ref, out_sems.at[0])
    out_store.start()
    attended_load.wait()
    norm = [s[:, i : i + 128] for s in (gain_sum, bias_sum) for i in range(0, width, 128)]
    norm = jnp.concatenate(norm, 0)
    high = norm.astype(LOW).astype(jnp.float32)
    norm = jnp.concatenate([high, norm - high], 0).astype(LOW)
    parts = [
        (0, dot_tn(normed_ref[...], grad_ref[...]).astype(LOW)),
        (3 * width, dot_tn(attended_ref[...], cot_ref[...]).astype(LOW)),
    ]
    planes, share, _ = keep_ref.shape
    core = lax.axis_index("core")
    stores = [out_store]
    for ref, target, core_at in ((send_ref, send_hbm_ref, 1 - core), (keep_ref, keep_hbm_ref, core)):
        order = share_order(width, planes, core_at)
        for lo, part in parts:
            part = dot_nn(order, part).astype(LOW).reshape(planes, share, part.shape[1])
            ref[:, :, lo : lo + part.shape[2]] = part
        ref[:, :, 4 * width :] = jnp.broadcast_to(norm[None], (planes,) + norm.shape)
        stores.append(pltpu.make_async_copy(ref, target, out_sems.at[len(stores)]))
        stores[-1].start()
    for store in stores:
        store.wait()


def share_order(width, planes, core):
    pair = width // (2 * planes * GRID)
    ring = planes // 4
    row = lax.broadcasted_iota(jnp.int32, (width // 2, width), 0)
    col = lax.broadcasted_iota(jnp.int32, (width // 2, width), 1)
    plane = row // (pair * GRID)
    spot = row // pair % GRID
    x = (plane // ring + here_x()) % 4
    y = (plane % ring + lax.axis_index("y")) % ring
    source = ((((x % 2 * GRID + spot) * ring + y) * 2 + x // 2) * 2 + core) * pair + row % pair
    return jnp.where(col == source, 1.0, 0.0).astype(LOW)


def here_x():
    return lax.axis_index("x_hi") * 2 + lax.axis_index("dp")


def split_norm(norm):
    high = norm.astype(LOW).astype(jnp.float32)
    return high, norm - high


def norm_total(refs, place, here):
    tiles = [ref[place].astype(jnp.float32) for ref in refs]
    tiles = [tile[:GRID] + tile[GRID:] for tile in tiles]
    total = None
    for at in range(len(refs)):
        back = lax.rem(here + len(refs) - at, len(refs))
        part = sum(jnp.where(back == s, tile, 0.0) for s, tile in enumerate(tiles))
        total = part if total is None else total + part
    return total


def core_sum_kernel(keep_ref, got_ref, *out_refs):
    ring = out_refs[0].shape[0]
    for s, out_ref in enumerate(out_refs):
        place = slice(s * ring, (s + 1) * ring)
        out_ref[...] = (
            keep_ref[place].astype(jnp.float32) + got_ref[place].astype(jnp.float32)
        ).astype(LOW)


def x_sum_kernel(*refs):
    refs, out_refs = refs[:4], refs[4:]
    main = refs[0].shape[2] - 128
    norm = norm_total(refs, (0, slice(None), slice(main, main + 128)), here_x())
    norm = jnp.concatenate(split_norm(norm), 0).astype(LOW)
    for t, out_ref in enumerate(out_refs):
        total = sum(ref[t, :, :main].astype(jnp.float32) for ref in refs)
        out_ref[:, :main] = total.astype(LOW)
        out_ref[:, main:] = norm


def y_sum_kernel(*refs):
    refs, out_ref = refs[:-1], refs[-1]
    rows, wide = refs[0].shape
    main = wide - 128
    total = sum(ref[:, :main].astype(jnp.float32) for ref in refs)
    norm = norm_total(refs, (slice(None), slice(main, wide)), lax.axis_index("y"))
    norm = [
        jnp.concatenate([part[i : i + 1] for i in range(GRID)], 1) for part in split_norm(norm)
    ]
    norm = jnp.concatenate(norm, 0).astype(LOW)
    out_ref[:, :, :main] = total.reshape(GRID, rows // GRID, main).astype(LOW)
    out_ref[:, :, main:] = jnp.broadcast_to(norm[None], (GRID,) + norm.shape)


def second_sum_kernel(shares_ref, qkv_ref, out_ref, norm_ref):
    total = jnp.sum(shares_ref[...].astype(jnp.float32), 0)
    width = norm_ref.shape[1]
    for row in range(total.shape[0]):
        qkv_ref[row * 3 * width : (row + 1) * 3 * width] = total[row, : 3 * width]
        out_ref[row * width : (row + 1) * width] = total[row, 3 * width : 4 * width]
    norm = total[0:1, 4 * width :] + total[1:2, 4 * width :]
    norm_ref[0:1, :] = norm[:, :width]
    norm_ref[1:2, :] = norm[:, width:]


def gather_kernel(*refs):
    slabs_ref, out_ref, copy_ref = refs[GRID:]
    spot = lax.axis_index("z")
    for shift in range(GRID):
        out_ref[lax.rem(spot + shift, GRID)] = refs[shift][...]
    copy_ref[...] = slabs_ref[...]


VMEM = pl.BlockSpec(memory_space=pltpu.VMEM)
ANY = pl.BlockSpec(memory_space=pl.ANY)
SHAPE = jax.ShapeDtypeStruct


def call(kernel, name, out_shape, *args, scratch=(), flops=0, moved=0, exps=0, limit=SMALL_LIMIT, in_specs=None, out_specs=None):
    return pl.pallas_call(
        kernel,
        out_shape=out_shape,
        in_specs=in_specs or [VMEM] * len(args),
        out_specs=out_specs or jax.tree.map(lambda _: VMEM, out_shape),
        scratch_shapes=list(scratch),
        compiler_params=pltpu.CompilerParams(vmem_limit_bytes=limit),
        cost_estimate=pl.CostEstimate(flops=flops, bytes_accessed=moved, transcendentals=exps),
        name=name,
    )(*args)


def forward(slabs, w_qkv, w_out, gain, bias):
    spots, columns, width = slabs.shape
    tokens = spots * columns
    flops = 2 * tokens * width * (4 * width + 2 * GRID * GRID * PACK)
    return call(
        forward_kernel,
        "forward",
        [SHAPE((columns, width), LOW)] * spots
        + [
            SHAPE((tokens, width), LOW),
            SHAPE((tokens, 3 * width), LOW),
            SHAPE((tokens, width), LOW),
        ],
        slabs,
        w_qkv,
        w_out,
        gain,
        bias,
        scratch=[pltpu.VMEM((columns // GRID, spots, GRID, width), jnp.float32)],
        flops=flops,
        moved=10 * 2**20,
        exps=tokens * HEADS * GRID * GRID,
        limit=VMEM_LIMIT,
    )


def backward(slabs, saved, w_qkv, w_out, gain, bias, planes):
    spots, columns, width = slabs.shape
    tokens = spots * columns
    share = width // (2 * planes)
    wide = 4 * width + 128
    flops = 2 * tokens * width * (9 * width + 5 * GRID * GRID * PACK)
    results = call(
        backward_kernel,
        "backward",
        [SHAPE(slabs.shape, LOW)]
        + [SHAPE((planes, share, wide), LOW)] * 2,
        slabs,
        *saved,
        w_qkv,
        w_out,
        gain,
        bias,
        scratch=[
            pltpu.VMEM((columns // GRID, spots, GRID, width), jnp.float32),
            pltpu.VMEM((tokens, width), LOW),
            pltpu.VMEM((tokens, width), LOW),
            pltpu.VMEM((tokens, 3 * width), LOW),
            pltpu.VMEM((tokens, width), LOW),
            pltpu.VMEM(slabs.shape, LOW),
            pltpu.VMEM(w_out.shape, LOW),
            pltpu.VMEM((tokens, 3 * width), LOW),
            pltpu.VMEM((tokens, width), LOW),
            pltpu.VMEM(w_qkv.shape, LOW),
            pltpu.VMEM((tokens, width), LOW),
            pltpu.VMEM(slabs.shape, LOW),
            pltpu.VMEM((planes, share, wide), LOW),
            pltpu.VMEM((planes, share, wide), LOW),
            pltpu.SemaphoreType.DMA((6,)),
            pltpu.SemaphoreType.DMA((3,)),
        ],
        in_specs=[ANY] * 6 + [VMEM] * 2,
        out_specs=[ANY] * 3,
        flops=flops,
        moved=16 * 2**20,
        exps=tokens * HEADS * GRID * GRID,
        limit=VMEM_LIMIT,
    )
    return results


def core_sum(keep, got):
    planes, rows, wide = keep.shape
    return call(core_sum_kernel, "core_sum", [SHAPE((planes // 4, rows, wide), LOW)] * 4, keep, got)


def x_sum(parts):
    ring, rows, wide = parts[0].shape
    return call(x_sum_kernel, "x_sum", [SHAPE((rows, wide), LOW)] * ring, *parts)


def y_sum(parts):
    rows, wide = parts[0].shape
    result = SHAPE((GRID, rows // GRID, wide - 128 + GRID * 128), LOW)
    return call(y_sum_kernel, "y_sum", result, *parts)


def second_sum(shares, width):
    _, rows, _ = shares.shape
    result = [
        SHAPE((rows * 3 * width,), jnp.float32),
        SHAPE((rows * width,), jnp.float32),
        SHAPE((2, width), jnp.float32),
    ]
    return call(second_sum_kernel, "second_sum", result, shares)


def gather_slabs(pieces, slabs):
    return call(gather_kernel, "gather_slabs", [SHAPE(slabs.shape, LOW)] * 2, *pieces, slabs)


def swap(value, axes):
    return lax.all_to_all(value, axes, split_axis=0, concat_axis=0, tiled=True)


def turn(value, shift):
    if shift % GRID == 0:
        return value
    return lax.ppermute(value, "z", [(a, (a + shift) % GRID) for a in range(GRID)])


def ring_parts(parts, axes, place=lambda at: at):
    size = len(parts)
    pairs = [[(place(a), place((a + s) % size)) for a in range(size)] for s in range(size)]
    return [part if s == 0 else lax.ppermute(part, axes, pairs[s]) for s, part in enumerate(parts)]


def body(latent, cotangent, w_qkv, w_out, norm_gain, norm_bias):
    width = latent.shape[-1]
    planes = lax.axis_size("dp") * lax.axis_size("y") * lax.axis_size("x_hi")
    gain = norm_gain.reshape(1, width)
    bias = norm_bias.reshape(1, width)
    slabs, cotangent = lax.optimization_barrier((swap(latent[0], "z"), cotangent[0]))
    cotangent = swap(cotangent, "z")
    results = forward(slabs, w_qkv, w_out, gain, bias)
    outs, saved = list(results[:GRID]), results[GRID:]
    outs = [turn(piece, -shift) for shift, piece in enumerate(outs)]
    grad_input, keep, send = backward(cotangent, saved, w_qkv, w_out, gain, bias, planes)
    outs[2:7], grad_input, keep, send = lax.optimization_barrier((outs[2:7], grad_input, keep, send))
    grad_input = swap(grad_input, "z")
    parts = core_sum(keep, lax.ppermute(send, "core", [(0, 1), (1, 0)]))
    parts = x_sum(ring_parts(parts, ("dp", "x_hi"), lambda x: x % 2 * 2 + x // 2))
    outs[1], outs[7], parts = lax.optimization_barrier((outs[1], outs[7], parts))
    shares = y_sum(ring_parts(parts, "y"))
    grad_input, shares = lax.optimization_barrier((grad_input, shares))
    grad_qkv, grad_out, grad_norm = second_sum(swap(shares, "z"), width)
    output, grad_input = gather_slabs(outs, grad_input)
    return (output[None], grad_input[None], grad_qkv, grad_out, grad_norm)


def solution(mesh):
    sizes = (mesh.shape["dp"], GRID, mesh.shape["space"] // GRID // 4, 2, 2)
    parts = jax.sharding.Mesh(mesh.devices.reshape(sizes), ("dp", "z", "y", "x_hi", "core"))
    space = ("z", "y", "x_hi", "core")
    in_specs = (P("dp", space, None, None), P("dp", space, None, None), P(), P(), P(), P())
    out_specs = (
        P("dp", space, None, None),
        P("dp", space, None, None),
        P(("dp",) + space),
        P(("dp",) + space),
        P(),
    )
    return jax.shard_map(body, mesh=parts, in_specs=in_specs, out_specs=out_specs, check_vma=False)
```

```python
import functools
import math

import jax
import jax.numpy as jnp
from jax import lax
from jax.experimental import pallas as pl
from jax.experimental.pallas import tpu as pltpu
from jax.sharding import PartitionSpec as P

HEADS = 16
GRID = 8
STEPS = 2
PACK = 4
UNROLL = 8
VMEM_LIMIT = 56 * 1024 * 1024
SMALL_LIMIT = 12 * 1024 * 1024
LOW = jnp.bfloat16


def dot_nn(a, b):
    return jnp.dot(a, b, preferred_element_type=jnp.float32)


def dot_nt(a, b):
    return lax.dot_general(a, b, (((1,), (1,)), ((), ())), preferred_element_type=jnp.float32)


def dot_tn(a, b):
    return lax.dot_general(a, b, (((0,), (0,)), ((), ())), preferred_element_type=jnp.float32)


def column_order(columns, back):
    inner = columns // GRID
    row = lax.broadcasted_iota(jnp.int32, (columns, columns), 0)
    col = lax.broadcasted_iota(jnp.int32, (columns, columns), 1)
    if back:
        row, col = col, row
    hit = (row // GRID == col % inner) & (row % GRID == col // inner)
    return jnp.where(hit, 1.0, 0.0).astype(LOW)


def to_windows(slabs_ref, cells_ref):
    spots, columns, width = slabs_ref.shape
    order = column_order(columns, False)
    for a in range(spots):
        moved = dot_nn(order, slabs_ref[a])
        cells_ref[:, a] = moved.reshape(columns // GRID, GRID, width)


def from_windows(cells_ref, a):
    inner, _, side, width = cells_ref.shape
    moved = cells_ref[:, a].reshape(inner * side, width).astype(LOW)
    return dot_nn(column_order(inner * side, True), moved).astype(LOW)


def step_rows(cells_ref, step):
    inner, spots, side, width = cells_ref.shape
    part = inner // STEPS
    return cells_ref[step * part : (step + 1) * part].reshape(part * spots * side, width)


def put_rows(cells_ref, step, value):
    inner, spots, side, width = cells_ref.shape
    part = inner // STEPS
    cells_ref[step * part : (step + 1) * part] = value.reshape(part, spots, side, width)


def norm_parts(values):
    center = jnp.mean(values, -1, keepdims=True)
    offset = values - center
    variance = jnp.mean(offset * offset, -1, keepdims=True)
    inverse = lax.rsqrt(variance + 1e-05)
    return offset * inverse, inverse


class Heads:
    def __init__(self, width):
        self.head_size = width // HEADS
        self.lanes = PACK * self.head_size
        self.cells = GRID * GRID
        self.factor = 1.0 / math.sqrt(self.head_size)
        shape = (PACK * self.cells, self.lanes)
        lane_head = lax.broadcasted_iota(jnp.int32, shape, 1) // self.head_size
        row_head = lax.broadcasted_iota(jnp.int32, shape, 0) // self.cells
        self.own = jnp.where(lane_head == row_head, 1.0, 0.0).astype(LOW)
        self.lane_of = lax.broadcasted_iota(jnp.int32, (self.cells, self.lanes), 1) // self.head_size
        self.slices = [slice(g * self.lanes, (g + 1) * self.lanes) for g in range(HEADS // PACK)]

    def columns(self, group):
        return slice(group * PACK * self.cells, (group + 1) * PACK * self.cells)

    def spread(self, part):
        return jnp.concatenate([part] * PACK, 0) * self.own

    def gather(self, wide):
        result = wide[: self.cells]
        for h in range(1, PACK):
            result = jnp.where(self.lane_of == h, wide[h * self.cells : (h + 1) * self.cells], result)
        return result

    def probs(self, keys, wide_q):
        scores = [dot_nt(k, q) * self.factor for k, q in zip(keys, wide_q)]
        weights = [jnp.exp(s - jnp.max(s, 0, keepdims=True)) for s in scores]
        return [e * (1.0 / jnp.sum(e, 0, keepdims=True)) for e in weights]


def forward_kernel(slabs_ref, w_qkv_ref, w_out_ref, gain_ref, bias_ref, *refs):
    piece_refs = refs[:GRID]
    latent_ref, proj_ref, attended_ref, probs_ref, cells_ref = refs[GRID:]
    width = w_out_ref.shape[0]
    rows = latent_ref.shape[0] // STEPS
    to_windows(slabs_ref, cells_ref)
    for step in range(STEPS):
        at = slice(step * rows, (step + 1) * rows)
        latent = step_rows(cells_ref, step)
        latent_ref[at, :] = latent.astype(LOW)
        scaled, _ = norm_parts(latent)
        normed = (scaled * gain_ref[...] + bias_ref[...]).astype(LOW)
        proj_ref[at, :] = dot_nn(normed, w_qkv_ref[...]).astype(LOW)
    heads = Heads(width)

    def window(w, carry):
        at = pl.ds(pl.multiple_of(w * heads.cells, heads.cells), heads.cells)
        keys = [proj_ref[at, width + s.start : width + s.stop] for s in heads.slices]
        wide_q = [heads.spread(proj_ref[at, s]) for s in heads.slices]
        probs = [p.astype(LOW) for p in heads.probs(keys, wide_q)]
        for g, (s, p) in enumerate(zip(heads.slices, probs)):
            probs_ref[at, heads.columns(g)] = p
            values = proj_ref[at, 2 * width + s.start : 2 * width + s.stop]
            attended_ref[at, s] = heads.gather(dot_tn(p, values)).astype(LOW)
        return carry

    lax.fori_loop(0, latent_ref.shape[0] // heads.cells, window, 0, unroll=UNROLL)
    for step in range(STEPS):
        at = slice(step * rows, (step + 1) * rows)
        value = step_rows(cells_ref, step) + dot_nn(attended_ref[at, :], w_out_ref[...])
        put_rows(cells_ref, step, value)
    spot = lax.axis_index("z")
    for shift in range(GRID):
        piece_refs[shift][...] = from_windows(cells_ref, lax.rem(spot + GRID - shift, GRID))


def backward_kernel(
    slabs_ref, latent_ref, proj_ref, attended_ref, probs_ref, w_qkv_ref, w_out_ref, gain_ref, bias_ref, *refs
):
    hbm_refs = (slabs_ref, w_out_ref, proj_ref, probs_ref, latent_ref, w_qkv_ref, attended_ref)
    out_hbm_ref, keep_hbm_ref, send_hbm_ref = refs[:3]
    cells_ref, cot_ref, heads_ref, grad_ref, normed_ref = refs[3:8]
    vmem_refs = refs[8:15]
    out_ref, keep_ref, send_ref, in_sems, out_sems = refs[15:]
    slabs_ref, w_out_ref, proj_ref, probs_ref, latent_ref, w_qkv_ref, attended_ref = vmem_refs
    loads = [
        pltpu.make_async_copy(source, target, in_sems.at[i])
        for i, (source, target) in enumerate(zip(hbm_refs, vmem_refs))
    ]
    for load in loads[:4]:
        load.start()
    slabs_load, w_out_load, proj_load, probs_load, latent_load, w_qkv_load, attended_load = loads
    width = w_out_ref.shape[0]
    rows = latent_ref.shape[0] // STEPS
    slabs_load.wait()
    for load in loads[4:]:
        load.start()
    to_windows(slabs_ref, cells_ref)
    w_out_load.wait()
    for step in range(STEPS):
        at = slice(step * rows, (step + 1) * rows)
        cot_ref[at, :] = step_rows(cells_ref, step).astype(LOW)
        heads_ref[at, :] = dot_nt(cot_ref[at, :], w_out_ref[...]).astype(LOW)
    proj_load.wait()
    probs_load.wait()
    heads = Heads(width)

    def window(w, carry):
        at = pl.ds(pl.multiple_of(w * heads.cells, heads.cells), heads.cells)
        keys = [proj_ref[at, width + s.start : width + s.stop] for s in heads.slices]
        values = [proj_ref[at, 2 * width + s.start : 2 * width + s.stop] for s in heads.slices]
        wide_q = [heads.spread(proj_ref[at, s]) for s in heads.slices]
        wide_g = [heads.spread(heads_ref[at, s]) for s in heads.slices]
        grad_probs = [dot_nt(v, g) for v, g in zip(values, wide_g)]
        probs_low = [probs_ref[at, heads.columns(g)] for g in range(len(heads.slices))]
        probs = [p.astype(jnp.float32) for p in probs_low]
        grad_scores = [
            (p * (d - jnp.sum(p * d, 0, keepdims=True))).astype(LOW)
            for p, d in zip(probs, grad_probs)
        ]
        for i, s in enumerate(heads.slices):
            grad_v = dot_nn(probs_low[i], wide_g[i])
            grad_k = dot_nn(grad_scores[i], wide_q[i]) * heads.factor
            grad_q = heads.gather(dot_tn(grad_scores[i], keys[i])) * heads.factor
            for j, part in enumerate((grad_q, grad_k, grad_v)):
                grad_ref[at, j * width + s.start : j * width + s.stop] = part.astype(LOW)
        return carry

    lax.fori_loop(0, latent_ref.shape[0] // heads.cells, window, 0, unroll=UNROLL)
    latent_load.wait()
    w_qkv_load.wait()
    gain_sum = jnp.zeros((1, width), jnp.float32)
    bias_sum = jnp.zeros((1, width), jnp.float32)
    for step in range(STEPS):
        at = slice(step * rows, (step + 1) * rows)
        scaled, inverse = norm_parts(latent_ref[at, :].astype(jnp.float32))
        normed_ref[at, :] = (scaled * gain_ref[...] + bias_ref[...]).astype(LOW)
        grad_normed = dot_nt(grad_ref[at, :], w_qkv_ref[...])
        gain_sum += jnp.sum(grad_normed * scaled, 0, keepdims=True)
        bias_sum += jnp.sum(grad_normed, 0, keepdims=True)
        grad_hat = grad_normed * gain_ref[...]
        value = step_rows(cells_ref, step) + inverse * (
            grad_hat
            - jnp.mean(grad_hat, -1, keepdims=True)
            - scaled * jnp.mean(grad_hat * scaled, -1, keepdims=True)
        )
        put_rows(cells_ref, step, value)
    for a in range(GRID):
        out_ref[a] = from_windows(cells_ref, a)
    out_store = pltpu.make_async_copy(out_ref, out_hbm_ref, out_sems.at[0])
    out_store.start()
    attended_load.wait()
    norm = [s[:, i : i + 128] for s in (gain_sum, bias_sum) for i in range(0, width, 128)]
    norm = jnp.concatenate(norm, 0)
    high = norm.astype(LOW).astype(jnp.float32)
    norm = jnp.concatenate([high, norm - high], 0).astype(LOW)
    parts = [
        (0, dot_tn(normed_ref[...], grad_ref[...]).astype(LOW)),
        (3 * width, dot_tn(attended_ref[...], cot_ref[...]).astype(LOW)),
    ]
    planes, share, _ = keep_ref.shape
    core = lax.axis_index("core")
    stores = [out_store]
    for ref, target, core_at in ((send_ref, send_hbm_ref, 1 - core), (keep_ref, keep_hbm_ref, core)):
        order = share_order(width, planes, core_at)
        for lo, part in parts:
            part = dot_nn(order, part).astype(LOW).reshape(planes, share, part.shape[1])
            ref[:, :, lo : lo + part.shape[2]] = part
        ref[:, :, 4 * width :] = jnp.broadcast_to(norm[None], (planes,) + norm.shape)
        stores.append(pltpu.make_async_copy(ref, target, out_sems.at[len(stores)]))
        stores[-1].start()
    for store in stores:
        store.wait()


def share_order(width, planes, core):
    pair = width // (2 * planes * GRID)
    ring = planes // 4
    row = lax.broadcasted_iota(jnp.int32, (width // 2, width), 0)
    col = lax.broadcasted_iota(jnp.int32, (width // 2, width), 1)
    plane = row // (pair * GRID)
    spot = row // pair % GRID
    x = (plane // ring + here_x()) % 4
    y = (plane % ring + lax.axis_index("y")) % ring
    source = ((((x % 2 * GRID + spot) * ring + y) * 2 + x // 2) * 2 + core) * pair + row % pair
    return jnp.where(col == source, 1.0, 0.0).astype(LOW)


def here_x():
    return lax.axis_index("x_hi") * 2 + lax.axis_index("dp")


def split_norm(norm):
    high = norm.astype(LOW).astype(jnp.float32)
    return high, norm - high


def norm_total(refs, place, here):
    tiles = [ref[place].astype(jnp.float32) for ref in refs]
    tiles = [tile[:GRID] + tile[GRID:] for tile in tiles]
    total = None
    for at in range(len(refs)):
        back = lax.rem(here + len(refs) - at, len(refs))
        part = sum(jnp.where(back == s, tile, 0.0) for s, tile in enumerate(tiles))
        total = part if total is None else total + part
    return total


def core_sum_kernel(keep_ref, got_ref, *out_refs):
    ring = out_refs[0].shape[0]
    for s, out_ref in enumerate(out_refs):
        place = slice(s * ring, (s + 1) * ring)
        out_ref[...] = (
            keep_ref[place].astype(jnp.float32) + got_ref[place].astype(jnp.float32)
        ).astype(LOW)


def x_sum_kernel(*refs):
    refs, out_refs = refs[:4], refs[4:]
    main = refs[0].shape[2] - 128
    norm = norm_total(refs, (0, slice(None), slice(main, main + 128)), here_x())
    norm = jnp.concatenate(split_norm(norm), 0).astype(LOW)
    for t, out_ref in enumerate(out_refs):
        total = sum(ref[t, :, :main].astype(jnp.float32) for ref in refs)
        out_ref[:, :main] = total.astype(LOW)
        out_ref[:, main:] = norm


def y_sum_kernel(*refs):
    refs, out_ref = refs[:-1], refs[-1]
    rows, wide = refs[0].shape
    main = wide - 128
    total = sum(ref[:, :main].astype(jnp.float32) for ref in refs)
    norm = norm_total(refs, (slice(None), slice(main, wide)), lax.axis_index("y"))
    norm = [
        jnp.concatenate([part[i : i + 1] for i in range(GRID)], 1) for part in split_norm(norm)
    ]
    norm = jnp.concatenate(norm, 0).astype(LOW)
    out_ref[:, :, :main] = total.reshape(GRID, rows // GRID, main).astype(LOW)
    out_ref[:, :, main:] = jnp.broadcast_to(norm[None], (GRID,) + norm.shape)


def second_sum_kernel(shares_ref, qkv_ref, out_ref, norm_ref):
    total = jnp.sum(shares_ref[...].astype(jnp.float32), 0)
    width = norm_ref.shape[1]
    for row in range(total.shape[0]):
        qkv_ref[row * 3 * width : (row + 1) * 3 * width] = total[row, : 3 * width]
        out_ref[row * width : (row + 1) * width] = total[row, 3 * width : 4 * width]
    norm = total[0:1, 4 * width :] + total[1:2, 4 * width :]
    norm_ref[0:1, :] = norm[:, :width]
    norm_ref[1:2, :] = norm[:, width:]


def gather_kernel(*refs):
    slabs_ref, out_ref, copy_ref = refs[GRID:]
    spot = lax.axis_index("z")
    for shift in range(GRID):
        out_ref[lax.rem(spot + shift, GRID)] = refs[shift][...]
    copy_ref[...] = slabs_ref[...]


VMEM = pl.BlockSpec(memory_space=pltpu.VMEM)
ANY = pl.BlockSpec(memory_space=pl.ANY)
SHAPE = jax.ShapeDtypeStruct


def call(kernel, name, out_shape, *args, scratch=(), flops=0, moved=0, exps=0, limit=SMALL_LIMIT, in_specs=None, out_specs=None):
    return pl.pallas_call(
        kernel,
        out_shape=out_shape,
        in_specs=in_specs or [VMEM] * len(args),
        out_specs=out_specs or jax.tree.map(lambda _: VMEM, out_shape),
        scratch_shapes=list(scratch),
        compiler_params=pltpu.CompilerParams(vmem_limit_bytes=limit),
        cost_estimate=pl.CostEstimate(flops=flops, bytes_accessed=moved, transcendentals=exps),
        name=name,
    )(*args)


def forward(slabs, w_qkv, w_out, gain, bias):
    spots, columns, width = slabs.shape
    tokens = spots * columns
    flops = 2 * tokens * width * (4 * width + 2 * GRID * GRID * PACK)
    return call(
        forward_kernel,
        "forward",
        [SHAPE((columns, width), LOW)] * spots
        + [
            SHAPE((tokens, width), LOW),
            SHAPE((tokens, 3 * width), LOW),
            SHAPE((tokens, width), LOW),
            SHAPE((tokens, HEADS * GRID * GRID), LOW),
        ],
        slabs,
        w_qkv,
        w_out,
        gain,
        bias,
        scratch=[pltpu.VMEM((columns // GRID, spots, GRID, width), jnp.float32)],
        flops=flops,
        moved=10 * 2**20,
        exps=tokens * HEADS * GRID * GRID,
        limit=VMEM_LIMIT,
    )


def backward(slabs, saved, w_qkv, w_out, gain, bias, planes):
    spots, columns, width = slabs.shape
    tokens = spots * columns
    share = width // (2 * planes)
    wide = 4 * width + 128
    flops = 2 * tokens * width * (9 * width + 5 * GRID * GRID * PACK)
    results = call(
        backward_kernel,
        "backward",
        [SHAPE(slabs.shape, LOW)]
        + [SHAPE((planes, share, wide), LOW)] * 2,
        slabs,
        *saved,
        w_qkv,
        w_out,
        gain,
        bias,
        scratch=[
            pltpu.VMEM((columns // GRID, spots, GRID, width), jnp.float32),
            pltpu.VMEM((tokens, width), LOW),
            pltpu.VMEM((tokens, width), LOW),
            pltpu.VMEM((tokens, 3 * width), LOW),
            pltpu.VMEM((tokens, width), LOW),
            pltpu.VMEM(slabs.shape, LOW),
            pltpu.VMEM(w_out.shape, LOW),
            pltpu.VMEM((tokens, 3 * width), LOW),
            pltpu.VMEM((tokens, HEADS * GRID * GRID), LOW),
            pltpu.VMEM((tokens, width), LOW),
            pltpu.VMEM(w_qkv.shape, LOW),
            pltpu.VMEM((tokens, width), LOW),
            pltpu.VMEM(slabs.shape, LOW),
            pltpu.VMEM((planes, share, wide), LOW),
            pltpu.VMEM((planes, share, wide), LOW),
            pltpu.SemaphoreType.DMA((7,)),
            pltpu.SemaphoreType.DMA((3,)),
        ],
        in_specs=[ANY] * 7 + [VMEM] * 2,
        out_specs=[ANY] * 3,
        flops=flops,
        moved=16 * 2**20,
        exps=tokens * HEADS * GRID * GRID,
        limit=VMEM_LIMIT,
    )
    return results


def core_sum(keep, got):
    planes, rows, wide = keep.shape
    return call(core_sum_kernel, "core_sum", [SHAPE((planes // 4, rows, wide), LOW)] * 4, keep, got)


def x_sum(parts):
    ring, rows, wide = parts[0].shape
    return call(x_sum_kernel, "x_sum", [SHAPE((rows, wide), LOW)] * ring, *parts)


def y_sum(parts):
    rows, wide = parts[0].shape
    result = SHAPE((GRID, rows // GRID, wide - 128 + GRID * 128), LOW)
    return call(y_sum_kernel, "y_sum", result, *parts)


def second_sum(shares, width):
    _, rows, _ = shares.shape
    result = [
        SHAPE((rows * 3 * width,), jnp.float32),
        SHAPE((rows * width,), jnp.float32),
        SHAPE((2, width), jnp.float32),
    ]
    return call(second_sum_kernel, "second_sum", result, shares)


def gather_slabs(pieces, slabs):
    return call(gather_kernel, "gather_slabs", [SHAPE(slabs.shape, LOW)] * 2, *pieces, slabs)


def swap(value, axes):
    return lax.all_to_all(value, axes, split_axis=0, concat_axis=0, tiled=True)


def turn(value, shift):
    if shift % GRID == 0:
        return value
    return lax.ppermute(value, "z", [(a, (a + shift) % GRID) for a in range(GRID)])


def ring_parts(parts, axes, place=lambda at: at):
    size = len(parts)
    pairs = [[(place(a), place((a + s) % size)) for a in range(size)] for s in range(size)]
    return [part if s == 0 else lax.ppermute(part, axes, pairs[s]) for s, part in enumerate(parts)]


def body(latent, cotangent, w_qkv, w_out, norm_gain, norm_bias):
    width = latent.shape[-1]
    planes = lax.axis_size("dp") * lax.axis_size("y") * lax.axis_size("x_hi")
    gain = norm_gain.reshape(1, width)
    bias = norm_bias.reshape(1, width)
    slabs, cotangent = lax.optimization_barrier((swap(latent[0], "z"), cotangent[0]))
    cotangent = swap(cotangent, "z")
    results = forward(slabs, w_qkv, w_out, gain, bias)
    outs, saved = list(results[:GRID]), results[GRID:]
    outs = [turn(piece, -shift) for shift, piece in enumerate(outs)]
    grad_input, keep, send = backward(cotangent, saved, w_qkv, w_out, gain, bias, planes)
    outs[2:7], grad_input, keep, send = lax.optimization_barrier((outs[2:7], grad_input, keep, send))
    grad_input = swap(grad_input, "z")
    parts = core_sum(keep, lax.ppermute(send, "core", [(0, 1), (1, 0)]))
    parts = x_sum(ring_parts(parts, ("dp", "x_hi"), lambda x: x % 2 * 2 + x // 2))
    shares = y_sum(ring_parts(parts, "y"))
    outs[1], outs[7], grad_input, shares = lax.optimization_barrier(
        (outs[1], outs[7], grad_input, shares)
    )
    grad_qkv, grad_out, grad_norm = second_sum(swap(shares, "z"), width)
    output, grad_input = gather_slabs(outs, grad_input)
    return (output[None], grad_input[None], grad_qkv, grad_out, grad_norm)


def solution(mesh):
    sizes = (mesh.shape["dp"], GRID, mesh.shape["space"] // GRID // 4, 2, 2)
    parts = jax.sharding.Mesh(mesh.devices.reshape(sizes), ("dp", "z", "y", "x_hi", "core"))
    space = ("z", "y", "x_hi", "core")
    in_specs = (P("dp", space, None, None), P("dp", space, None, None), P(), P(), P(), P())
    out_specs = (
        P("dp", space, None, None),
        P("dp", space, None, None),
        P(("dp",) + space),
        P(("dp",) + space),
        P(),
    )
    return jax.shard_map(body, mesh=parts, in_specs=in_specs, out_specs=out_specs, check_vma=False)
```

```python
import functools
import math

import jax
import jax.numpy as jnp
from jax import lax
from jax.experimental import pallas as pl
from jax.experimental.pallas import tpu as pltpu
from jax.sharding import PartitionSpec as P

HEADS = 16
GRID = 8
STEPS = 2
PACK = 4
UNROLL = 8
VMEM_LIMIT = 56 * 1024 * 1024
SMALL_LIMIT = 12 * 1024 * 1024
LOW = jnp.bfloat16


def dot_nn(a, b):
    return jnp.dot(a, b, preferred_element_type=jnp.float32)


def dot_nt(a, b):
    return lax.dot_general(a, b, (((1,), (1,)), ((), ())), preferred_element_type=jnp.float32)


def dot_tn(a, b):
    return lax.dot_general(a, b, (((0,), (0,)), ((), ())), preferred_element_type=jnp.float32)


def column_order(columns, back):
    inner = columns // GRID
    row = lax.broadcasted_iota(jnp.int32, (columns, columns), 0)
    col = lax.broadcasted_iota(jnp.int32, (columns, columns), 1)
    if back:
        row, col = col, row
    hit = (row // GRID == col % inner) & (row % GRID == col // inner)
    return jnp.where(hit, 1.0, 0.0).astype(LOW)


def to_windows(slabs_ref, cells_ref):
    spots, columns, width = slabs_ref.shape
    order = column_order(columns, False)
    for a in range(spots):
        moved = dot_nn(order, slabs_ref[a])
        cells_ref[:, a] = moved.reshape(columns // GRID, GRID, width)


def from_windows(cells_ref, a):
    inner, _, side, width = cells_ref.shape
    moved = cells_ref[:, a].reshape(inner * side, width).astype(LOW)
    return dot_nn(column_order(inner * side, True), moved).astype(LOW)


def step_rows(cells_ref, step):
    inner, spots, side, width = cells_ref.shape
    part = inner // STEPS
    return cells_ref[step * part : (step + 1) * part].reshape(part * spots * side, width)


def put_rows(cells_ref, step, value):
    inner, spots, side, width = cells_ref.shape
    part = inner // STEPS
    cells_ref[step * part : (step + 1) * part] = value.reshape(part, spots, side, width)


def norm_parts(values):
    center = jnp.mean(values, -1, keepdims=True)
    offset = values - center
    variance = jnp.mean(offset * offset, -1, keepdims=True)
    inverse = lax.rsqrt(variance + 1e-05)
    return offset * inverse, inverse


class Heads:
    def __init__(self, width):
        self.head_size = width // HEADS
        self.lanes = PACK * self.head_size
        self.cells = GRID * GRID
        self.factor = 1.0 / math.sqrt(self.head_size)
        shape = (PACK * self.cells, self.lanes)
        lane_head = lax.broadcasted_iota(jnp.int32, shape, 1) // self.head_size
        row_head = lax.broadcasted_iota(jnp.int32, shape, 0) // self.cells
        self.own = jnp.where(lane_head == row_head, 1.0, 0.0).astype(LOW)
        self.lane_of = lax.broadcasted_iota(jnp.int32, (self.cells, self.lanes), 1) // self.head_size
        self.slices = [slice(g * self.lanes, (g + 1) * self.lanes) for g in range(HEADS // PACK)]

    def columns(self, group):
        return slice(group * PACK * self.cells, (group + 1) * PACK * self.cells)

    def spread(self, part):
        return jnp.concatenate([part] * PACK, 0) * self.own

    def gather(self, wide):
        result = wide[: self.cells]
        for h in range(1, PACK):
            result = jnp.where(self.lane_of == h, wide[h * self.cells : (h + 1) * self.cells], result)
        return result

    def probs(self, keys, wide_q):
        scores = [dot_nt(k, q) * self.factor for k, q in zip(keys, wide_q)]
        weights = [jnp.exp(s - jnp.max(s, 0, keepdims=True)) for s in scores]
        return [e * (1.0 / jnp.sum(e, 0, keepdims=True)) for e in weights]


def forward_kernel(slabs_ref, w_qkv_ref, w_out_ref, gain_ref, bias_ref, *refs):
    piece_refs = refs[:GRID]
    saved_refs, cells_ref = refs[GRID : GRID + 4], refs[GRID + 4]
    latent_ref, proj_ref, attended_ref, probs_ref, sems = refs[GRID + 5 :]
    stores = [
        pltpu.make_async_copy(source, target, sems.at[i])
        for i, (source, target) in enumerate(zip(refs[GRID + 5 :], saved_refs))
    ]
    width = w_out_ref.shape[0]
    rows = latent_ref.shape[0] // STEPS
    to_windows(slabs_ref, cells_ref)
    for step in range(STEPS):
        at = slice(step * rows, (step + 1) * rows)
        latent = step_rows(cells_ref, step)
        latent_ref[at, :] = latent.astype(LOW)
        scaled, _ = norm_parts(latent)
        normed = (scaled * gain_ref[...] + bias_ref[...]).astype(LOW)
        proj_ref[at, :] = dot_nn(normed, w_qkv_ref[...]).astype(LOW)
    stores[0].start()
    stores[1].start()
    heads = Heads(width)

    def window(w, carry):
        at = pl.ds(pl.multiple_of(w * heads.cells, heads.cells), heads.cells)
        keys = [proj_ref[at, width + s.start : width + s.stop] for s in heads.slices]
        wide_q = [heads.spread(proj_ref[at, s]) for s in heads.slices]
        probs = [p.astype(LOW) for p in heads.probs(keys, wide_q)]
        for g, (s, p) in enumerate(zip(heads.slices, probs)):
            probs_ref[at, heads.columns(g)] = p
            values = proj_ref[at, 2 * width + s.start : 2 * width + s.stop]
            attended_ref[at, s] = heads.gather(dot_tn(p, values)).astype(LOW)
        return carry

    lax.fori_loop(0, latent_ref.shape[0] // heads.cells, window, 0, unroll=UNROLL)
    stores[2].start()
    stores[3].start()
    for step in range(STEPS):
        at = slice(step * rows, (step + 1) * rows)
        value = step_rows(cells_ref, step) + dot_nn(attended_ref[at, :], w_out_ref[...])
        put_rows(cells_ref, step, value)
    spot = lax.axis_index("z")
    for shift in range(GRID):
        piece_refs[shift][...] = from_windows(cells_ref, lax.rem(spot + GRID - shift, GRID))
    for store in stores:
        store.wait()


def backward_kernel(
    slabs_ref, latent_ref, proj_ref, attended_ref, probs_ref, w_qkv_ref, w_out_ref, gain_ref, bias_ref, *refs
):
    hbm_refs = (slabs_ref, w_out_ref, proj_ref, probs_ref, latent_ref, w_qkv_ref, attended_ref)
    out_hbm_ref, keep_hbm_ref, send_hbm_ref = refs[:3]
    cells_ref, cot_ref, heads_ref, grad_ref, normed_ref = refs[3:8]
    vmem_refs = refs[8:15]
    out_ref, keep_ref, send_ref, in_sems, out_sems = refs[15:]
    slabs_ref, w_out_ref, proj_ref, probs_ref, latent_ref, w_qkv_ref, attended_ref = vmem_refs
    loads = [
        pltpu.make_async_copy(source, target, in_sems.at[i])
        for i, (source, target) in enumerate(zip(hbm_refs, vmem_refs))
    ]
    for load in loads[:4]:
        load.start()
    slabs_load, w_out_load, proj_load, probs_load, latent_load, w_qkv_load, attended_load = loads
    width = w_out_ref.shape[0]
    rows = latent_ref.shape[0] // STEPS
    slabs_load.wait()
    for load in loads[4:]:
        load.start()
    to_windows(slabs_ref, cells_ref)
    w_out_load.wait()
    for step in range(STEPS):
        at = slice(step * rows, (step + 1) * rows)
        cot_ref[at, :] = step_rows(cells_ref, step).astype(LOW)
        heads_ref[at, :] = dot_nt(cot_ref[at, :], w_out_ref[...]).astype(LOW)
    proj_load.wait()
    probs_load.wait()
    heads = Heads(width)

    def window(w, carry):
        at = pl.ds(pl.multiple_of(w * heads.cells, heads.cells), heads.cells)
        keys = [proj_ref[at, width + s.start : width + s.stop] for s in heads.slices]
        values = [proj_ref[at, 2 * width + s.start : 2 * width + s.stop] for s in heads.slices]
        wide_q = [heads.spread(proj_ref[at, s]) for s in heads.slices]
        wide_g = [heads.spread(heads_ref[at, s]) for s in heads.slices]
        grad_probs = [dot_nt(v, g) for v, g in zip(values, wide_g)]
        probs_low = [probs_ref[at, heads.columns(g)] for g in range(len(heads.slices))]
        probs = [p.astype(jnp.float32) for p in probs_low]
        grad_scores = [
            (p * (d - jnp.sum(p * d, 0, keepdims=True))).astype(LOW)
            for p, d in zip(probs, grad_probs)
        ]
        for i, s in enumerate(heads.slices):
            grad_v = dot_nn(probs_low[i], wide_g[i])
            grad_k = dot_nn(grad_scores[i], wide_q[i]) * heads.factor
            grad_q = heads.gather(dot_tn(grad_scores[i], keys[i])) * heads.factor
            for j, part in enumerate((grad_q, grad_k, grad_v)):
                grad_ref[at, j * width + s.start : j * width + s.stop] = part.astype(LOW)
        return carry

    lax.fori_loop(0, latent_ref.shape[0] // heads.cells, window, 0, unroll=UNROLL)
    latent_load.wait()
    w_qkv_load.wait()
    gain_sum = jnp.zeros((1, width), jnp.float32)
    bias_sum = jnp.zeros((1, width), jnp.float32)
    for step in range(STEPS):
        at = slice(step * rows, (step + 1) * rows)
        scaled, inverse = norm_parts(latent_ref[at, :].astype(jnp.float32))
        normed_ref[at, :] = (scaled * gain_ref[...] + bias_ref[...]).astype(LOW)
        grad_normed = dot_nt(grad_ref[at, :], w_qkv_ref[...])
        gain_sum += jnp.sum(grad_normed * scaled, 0, keepdims=True)
        bias_sum += jnp.sum(grad_normed, 0, keepdims=True)
        grad_hat = grad_normed * gain_ref[...]
        value = step_rows(cells_ref, step) + inverse * (
            grad_hat
            - jnp.mean(grad_hat, -1, keepdims=True)
            - scaled * jnp.mean(grad_hat * scaled, -1, keepdims=True)
        )
        put_rows(cells_ref, step, value)
    for a in range(GRID):
        out_ref[a] = from_windows(cells_ref, a)
    out_store = pltpu.make_async_copy(out_ref, out_hbm_ref, out_sems.at[0])
    out_store.start()
    attended_load.wait()
    norm = [s[:, i : i + 128] for s in (gain_sum, bias_sum) for i in range(0, width, 128)]
    norm = jnp.concatenate(norm, 0)
    high = norm.astype(LOW).astype(jnp.float32)
    norm = jnp.concatenate([high, norm - high], 0).astype(LOW)
    parts = [
        (0, dot_tn(normed_ref[...], grad_ref[...]).astype(LOW)),
        (3 * width, dot_tn(attended_ref[...], cot_ref[...]).astype(LOW)),
    ]
    planes, share, _ = keep_ref.shape
    core = lax.axis_index("core")
    stores = [out_store]
    for ref, target, core_at in ((send_ref, send_hbm_ref, 1 - core), (keep_ref, keep_hbm_ref, core)):
        order = share_order(width, planes, core_at)
        for lo, part in parts:
            part = dot_nn(order, part).astype(LOW).reshape(planes, share, part.shape[1])
            ref[:, :, lo : lo + part.shape[2]] = part
        ref[:, :, 4 * width :] = jnp.broadcast_to(norm[None], (planes,) + norm.shape)
        stores.append(pltpu.make_async_copy(ref, target, out_sems.at[len(stores)]))
        stores[-1].start()
    for store in stores:
        store.wait()


def share_order(width, planes, core):
    pair = width // (2 * planes * GRID)
    ring = planes // 4
    row = lax.broadcasted_iota(jnp.int32, (width // 2, width), 0)
    col = lax.broadcasted_iota(jnp.int32, (width // 2, width), 1)
    plane = row // (pair * GRID)
    spot = row // pair % GRID
    x = (plane // ring + here_x()) % 4
    y = (plane % ring + lax.axis_index("y")) % ring
    source = ((((x % 2 * GRID + spot) * ring + y) * 2 + x // 2) * 2 + core) * pair + row % pair
    return jnp.where(col == source, 1.0, 0.0).astype(LOW)


def here_x():
    return lax.axis_index("x_hi") * 2 + lax.axis_index("dp")


def split_norm(norm):
    high = norm.astype(LOW).astype(jnp.float32)
    return high, norm - high


def norm_total(refs, place, here):
    tiles = [ref[place].astype(jnp.float32) for ref in refs]
    tiles = [tile[:GRID] + tile[GRID:] for tile in tiles]
    total = None
    for at in range(len(refs)):
        back = lax.rem(here + len(refs) - at, len(refs))
        part = sum(jnp.where(back == s, tile, 0.0) for s, tile in enumerate(tiles))
        total = part if total is None else total + part
    return total


def core_sum_kernel(keep_ref, got_ref, *out_refs):
    ring = out_refs[0].shape[0]
    for s, out_ref in enumerate(out_refs):
        place = slice(s * ring, (s + 1) * ring)
        out_ref[...] = (
            keep_ref[place].astype(jnp.float32) + got_ref[place].astype(jnp.float32)
        ).astype(LOW)


def x_sum_kernel(*refs):
    refs, out_refs = refs[:4], refs[4:]
    main = refs[0].shape[2] - 128
    norm = norm_total(refs, (0, slice(None), slice(main, main + 128)), here_x())
    norm = jnp.concatenate(split_norm(norm), 0).astype(LOW)
    for t, out_ref in enumerate(out_refs):
        total = sum(ref[t, :, :main].astype(jnp.float32) for ref in refs)
        out_ref[:, :main] = total.astype(LOW)
        out_ref[:, main:] = norm


def y_sum_kernel(*refs):
    refs, out_ref = refs[:-1], refs[-1]
    rows, wide = refs[0].shape
    main = wide - 128
    total = sum(ref[:, :main].astype(jnp.float32) for ref in refs)
    norm = norm_total(refs, (slice(None), slice(main, wide)), lax.axis_index("y"))
    norm = [
        jnp.concatenate([part[i : i + 1] for i in range(GRID)], 1) for part in split_norm(norm)
    ]
    norm = jnp.concatenate(norm, 0).astype(LOW)
    out_ref[:, :, :main] = total.reshape(GRID, rows // GRID, main).astype(LOW)
    out_ref[:, :, main:] = jnp.broadcast_to(norm[None], (GRID,) + norm.shape)


def second_sum_kernel(shares_ref, qkv_ref, out_ref, norm_ref):
    total = jnp.sum(shares_ref[...].astype(jnp.float32), 0)
    width = norm_ref.shape[1]
    for row in range(total.shape[0]):
        qkv_ref[row * 3 * width : (row + 1) * 3 * width] = total[row, : 3 * width]
        out_ref[row * width : (row + 1) * width] = total[row, 3 * width : 4 * width]
    norm = total[0:1, 4 * width :] + total[1:2, 4 * width :]
    norm_ref[0:1, :] = norm[:, :width]
    norm_ref[1:2, :] = norm[:, width:]


def gather_kernel(*refs):
    slabs_ref, out_ref, copy_ref = refs[GRID:]
    spot = lax.axis_index("z")
    for shift in range(GRID):
        out_ref[lax.rem(spot + shift, GRID)] = refs[shift][...]
    copy_ref[...] = slabs_ref[...]


VMEM = pl.BlockSpec(memory_space=pltpu.VMEM)
ANY = pl.BlockSpec(memory_space=pl.ANY)
SHAPE = jax.ShapeDtypeStruct


def call(kernel, name, out_shape, *args, scratch=(), flops=0, moved=0, exps=0, limit=SMALL_LIMIT, in_specs=None, out_specs=None):
    return pl.pallas_call(
        kernel,
        out_shape=out_shape,
        in_specs=in_specs or [VMEM] * len(args),
        out_specs=out_specs or jax.tree.map(lambda _: VMEM, out_shape),
        scratch_shapes=list(scratch),
        compiler_params=pltpu.CompilerParams(vmem_limit_bytes=limit),
        cost_estimate=pl.CostEstimate(flops=flops, bytes_accessed=moved, transcendentals=exps),
        name=name,
    )(*args)


def forward(slabs, w_qkv, w_out, gain, bias):
    spots, columns, width = slabs.shape
    tokens = spots * columns
    flops = 2 * tokens * width * (4 * width + 2 * GRID * GRID * PACK)
    return call(
        forward_kernel,
        "forward",
        [SHAPE((columns, width), LOW)] * spots
        + [
            SHAPE((tokens, width), LOW),
            SHAPE((tokens, 3 * width), LOW),
            SHAPE((tokens, width), LOW),
            SHAPE((tokens, HEADS * GRID * GRID), LOW),
        ],
        slabs,
        w_qkv,
        w_out,
        gain,
        bias,
        scratch=[
            pltpu.VMEM((columns // GRID, spots, GRID, width), jnp.float32),
            pltpu.VMEM((tokens, width), LOW),
            pltpu.VMEM((tokens, 3 * width), LOW),
            pltpu.VMEM((tokens, width), LOW),
            pltpu.VMEM((tokens, HEADS * GRID * GRID), LOW),
            pltpu.SemaphoreType.DMA((4,)),
        ],
        out_specs=[VMEM] * spots + [ANY] * 4,
        flops=flops,
        moved=10 * 2**20,
        exps=tokens * HEADS * GRID * GRID,
        limit=VMEM_LIMIT,
    )


def backward(slabs, saved, w_qkv, w_out, gain, bias, planes):
    spots, columns, width = slabs.shape
    tokens = spots * columns
    share = width // (2 * planes)
    wide = 4 * width + 128
    flops = 2 * tokens * width * (9 * width + 5 * GRID * GRID * PACK)
    results = call(
        backward_kernel,
        "backward",
        [SHAPE(slabs.shape, LOW)]
        + [SHAPE((planes, share, wide), LOW)] * 2,
        slabs,
        *saved,
        w_qkv,
        w_out,
        gain,
        bias,
        scratch=[
            pltpu.VMEM((columns // GRID, spots, GRID, width), jnp.float32),
            pltpu.VMEM((tokens, width), LOW),
            pltpu.VMEM((tokens, width), LOW),
            pltpu.VMEM((tokens, 3 * width), LOW),
            pltpu.VMEM((tokens, width), LOW),
            pltpu.VMEM(slabs.shape, LOW),
            pltpu.VMEM(w_out.shape, LOW),
            pltpu.VMEM((tokens, 3 * width), LOW),
            pltpu.VMEM((tokens, HEADS * GRID * GRID), LOW),
            pltpu.VMEM((tokens, width), LOW),
            pltpu.VMEM(w_qkv.shape, LOW),
            pltpu.VMEM((tokens, width), LOW),
            pltpu.VMEM(slabs.shape, LOW),
            pltpu.VMEM((planes, share, wide), LOW),
            pltpu.VMEM((planes, share, wide), LOW),
            pltpu.SemaphoreType.DMA((7,)),
            pltpu.SemaphoreType.DMA((3,)),
        ],
        in_specs=[ANY] * 7 + [VMEM] * 2,
        out_specs=[ANY] * 3,
        flops=flops,
        moved=16 * 2**20,
        exps=tokens * HEADS * GRID * GRID,
        limit=VMEM_LIMIT,
    )
    return results


def core_sum(keep, got):
    planes, rows, wide = keep.shape
    return call(core_sum_kernel, "core_sum", [SHAPE((planes // 4, rows, wide), LOW)] * 4, keep, got)


def x_sum(parts):
    ring, rows, wide = parts[0].shape
    return call(x_sum_kernel, "x_sum", [SHAPE((rows, wide), LOW)] * ring, *parts)


def y_sum(parts):
    rows, wide = parts[0].shape
    result = SHAPE((GRID, rows // GRID, wide - 128 + GRID * 128), LOW)
    return call(y_sum_kernel, "y_sum", result, *parts)


def second_sum(shares, width):
    _, rows, _ = shares.shape
    result = [
        SHAPE((rows * 3 * width,), jnp.float32),
        SHAPE((rows * width,), jnp.float32),
        SHAPE((2, width), jnp.float32),
    ]
    return call(second_sum_kernel, "second_sum", result, shares)


def gather_slabs(pieces, slabs):
    return call(gather_kernel, "gather_slabs", [SHAPE(slabs.shape, LOW)] * 2, *pieces, slabs)


def swap(value, axes):
    return lax.all_to_all(value, axes, split_axis=0, concat_axis=0, tiled=True)


def turn(value, shift):
    if shift % GRID == 0:
        return value
    return lax.ppermute(value, "z", [(a, (a + shift) % GRID) for a in range(GRID)])


def ring_parts(parts, axes, place=lambda at: at):
    size = len(parts)
    pairs = [[(place(a), place((a + s) % size)) for a in range(size)] for s in range(size)]
    return [part if s == 0 else lax.ppermute(part, axes, pairs[s]) for s, part in enumerate(parts)]


def body(latent, cotangent, w_qkv, w_out, norm_gain, norm_bias):
    width = latent.shape[-1]
    planes = lax.axis_size("dp") * lax.axis_size("y") * lax.axis_size("x_hi")
    gain = norm_gain.reshape(1, width)
    bias = norm_bias.reshape(1, width)
    slabs, cotangent = lax.optimization_barrier((swap(latent[0], "z"), cotangent[0]))
    cotangent = swap(cotangent, "z")
    results = forward(slabs, w_qkv, w_out, gain, bias)
    outs, saved = list(results[:GRID]), results[GRID:]
    outs = [turn(piece, -shift) for shift, piece in enumerate(outs)]
    grad_input, keep, send = backward(cotangent, saved, w_qkv, w_out, gain, bias, planes)
    outs[2:7], grad_input, keep, send = lax.optimization_barrier((outs[2:7], grad_input, keep, send))
    grad_input = swap(grad_input, "z")
    parts = core_sum(keep, lax.ppermute(send, "core", [(0, 1), (1, 0)]))
    parts = x_sum(ring_parts(parts, ("dp", "x_hi"), lambda x: x % 2 * 2 + x // 2))
    shares = y_sum(ring_parts(parts, "y"))
    outs[1], outs[7], grad_input, shares = lax.optimization_barrier(
        (outs[1], outs[7], grad_input, shares)
    )
    grad_qkv, grad_out, grad_norm = second_sum(swap(shares, "z"), width)
    output, grad_input = gather_slabs(outs, grad_input)
    return (output[None], grad_input[None], grad_qkv, grad_out, grad_norm)


def solution(mesh):
    sizes = (mesh.shape["dp"], GRID, mesh.shape["space"] // GRID // 4, 2, 2)
    parts = jax.sharding.Mesh(mesh.devices.reshape(sizes), ("dp", "z", "y", "x_hi", "core"))
    space = ("z", "y", "x_hi", "core")
    in_specs = (P("dp", space, None, None), P("dp", space, None, None), P(), P(), P(), P())
    out_specs = (
        P("dp", space, None, None),
        P("dp", space, None, None),
        P(("dp",) + space),
        P(("dp",) + space),
        P(),
    )
    return jax.shard_map(body, mesh=parts, in_specs=in_specs, out_specs=out_specs, check_vma=False)
```
